32 devices in a mesh: span: 8 (over z, core), chord: 4 (over y, x).
Axes of the slice: x: 2, y: 2, z: 4, core: 2. Of those that a mesh axis runs over, the one named last changes fastest.
Arguments:
- flow_state: float32 [2, 5, 32, 256, 128], P(None, None, 'span', 'chord'), may hold values from -6 to 6
- jacobians: bfloat16 [7, 5, 5, 32, 256, 128], P(None, None, None, 'span', 'chord'), may hold values from -1 to 1
- beam_state: float32 [2, 12, 2048], P(None, None, 'span'), may hold values from -6 to 6
- stiffness: float32 [5, 12, 12, 2048], P(None, None, None, 'span'), may hold values from -0.75 to 0.75
- motion_map: float32 [5, 12, 32, 256], P(None, None, 'span', 'chord'), may hold values from -1.75 to 1.75
- load_map: float32 [12, 5, 32, 256], P(None, None, 'span', 'chord'), may hold values from -2.5 to 2.5
- surface_mask: int32 [32, 256], P('span', 'chord'), may hold values 0 or 1
- station_of: int32 [32, 256], P('span', 'chord'), may hold values from 0 to 2047
Outputs:
- flow_image: float32 [2, 5, 32, 256, 128], P(None, None, 'span', 'chord')
- beam_image: float32 [2, 12, 2048], P(None, None, 'span')
The draws below stay inside these ranges and needn't reach their ends.
All inputs are finite; a program needn't handle non-finite values. No bound on the sum of `surface_mask` on one device may be relied on, other than what follows from the above.
Results may differ from the reference program's by a relative error of at most 0.0003.
Values sent between devices are 32-bit elements; how exact they have to be, the bound alone decides.
No kernel may reach another device: no remote copies, remote signals or barrier semaphores. Data moves between devices by JAX's collectives and lax.ppermute only.
A program may use at most 192 MiB of HBM per device.

```python
import jax
import jax.numpy as jnp
from jax import lax

NVAR = 5
NDOF = 12
NCELL = 128
NVEC = 2
STA_DEV = 256
NS = 32
NC = 256
STATIONS = 2048
STA_BLADE = 512


def place_ends(entries, key, smallest, high):
    index_at = [jax.random.randint(jax.random.fold_in(key, axis), (), 0, length) for axis, length in enumerate(entries.shape)]
    longest = entries.shape.index(max(entries.shape))
    beside = index_at[:longest] + [(index_at[longest] + 1) % entries.shape[longest]] + index_at[longest + 1:]
    return entries.at[tuple(index_at)].set(smallest).at[tuple(beside)].set(high)


def steps_of(key, extent, shards, smallest, high):
    loudness, own = 1.0, jax.random.fold_in(key, 6)
    for axis_at, shards_of in shards:
        heights = jnp.exp(jax.random.uniform(jax.random.fold_in(own, axis_at), (shards_of,), jnp.float32, smallest / len(shards), high / len(shards)))
        loudness = loudness * jnp.repeat(heights, extent[axis_at] // shards_of).reshape([-1 if axis == axis_at else 1 for axis in range(len(extent))])
    return loudness


def scatter_about(own_key, extent, scale, limit, shards=(), kind=jnp.bfloat16):
    array = scale * jax.random.normal(own_key, extent, jnp.float32)
    if shards:
        array = array * steps_of(own_key, extent, shards, -0.22, 0.18)
    return jnp.clip(array, -limit, limit).astype(kind)


def setup_inputs(seed: int = 0) -> dict:
    splits = jax.random.split(jax.random.key(seed), 9)
    return {
        "flow_state": scatter_about(splits[0], (NVEC, NVAR, NS, NC, NCELL), 1.0, 6.0, ((2, 8), (3, 4)), jnp.float32),
        "jacobians": scatter_about(splits[1], (7, NVAR, NVAR, NS, NC, NCELL), 35 ** -0.5, 1.0, ((3, 8), (4, 4))),
        "beam_state": scatter_about(splits[2], (NVEC, NDOF, STATIONS), 1.0, 6.0, ((2, 8),), jnp.float32),
        "stiffness": scatter_about(splits[3], (5, NDOF, NDOF, STATIONS), 60 ** -0.5, 0.75, ((3, 8),), jnp.float32),
        "motion_map": scatter_about(splits[4], (NVAR, NDOF, NS, NC), 12 ** -0.5, 1.75, ((2, 8), (3, 4)), jnp.float32),
        "load_map": scatter_about(splits[5], (NDOF, NVAR, NS, NC), 5 ** -0.5, 2.5, ((2, 8), (3, 4)), jnp.float32),
        "surface_mask": place_ends((jax.random.randint(splits[6], (NS, NC), 0, 3) < 1).astype(jnp.int32), jax.random.fold_in(splits[6], 1), 0, 1),
        "station_of": place_ends(jax.random.randint(splits[7], (NS, NC), 0, STATIONS), jax.random.fold_in(splits[7], 1), 0, STATIONS - 1).astype(jnp.int32),
    }


def neighbour(padded, e):
    if e == 0:
        return padded[:, :, 1:-1, 1:-1, 1:-1]
    if e == 1:
        return padded[:, :, :-2, 1:-1, 1:-1]
    if e == 2:
        return padded[:, :, 2:, 1:-1, 1:-1]
    if e == 3:
        return padded[:, :, 1:-1, :-2, 1:-1]
    if e == 4:
        return padded[:, :, 1:-1, 2:, 1:-1]
    if e == 5:
        return padded[:, :, 1:-1, 1:-1, :-2]
    return padded[:, :, 1:-1, 1:-1, 2:]


def reference(flow_state, jacobians, beam_state, stiffness, motion_map, load_map, surface_mask, station_of):
    padded = jnp.pad(flow_state, ((0, 0), (0, 0), (1, 1), (1, 1), (1, 1)))
    rows = [jnp.zeros(flow_state[:, 0].shape, jnp.float32) for a in range(NVAR)]
    for e in range(7):
        near = neighbour(padded, e)
        for a in range(NVAR):
            for b in range(NVAR):
                rows[a] = rows[a] + jacobians[e, a, b].astype(jnp.float32) * near[:, b]
    stencil = jnp.stack(rows, axis=1)
    maskf = surface_mask.astype(jnp.float32)
    index = station_of.reshape(-1).astype(jnp.int32)
    looked = jnp.take(beam_state, index, axis=2).reshape(NVEC, NDOF, NS, NC)
    coupled = jnp.einsum('ajrc,vjrc->varc', motion_map, looked, precision=lax.Precision.HIGHEST) * maskf
    flow_image = jnp.concatenate([stencil[..., :1] + coupled[..., None], stencil[..., 1:]], axis=4)
    surf = flow_state[..., 0]
    wall_load = jnp.einsum('jarc,varc->vjrc', load_map, surf, precision=lax.Precision.HIGHEST) * maskf
    flat = wall_load.reshape(NVEC * NDOF, NS * NC).T
    loads = jax.ops.segment_sum(flat, index, num_segments=STATIONS).T.reshape(NVEC, NDOF, STATIONS)
    shifted = jnp.pad(beam_state, ((0, 0), (0, 0), (2, 2)))
    place = jnp.arange(STATIONS, dtype=jnp.int32)
    offset = STA_DEV // 2
    band = jnp.zeros((NVEC, NDOF, STATIONS), jnp.float32)
    for d in range(5):
        other = place + (d - 2)
        same = ((other + offset) // STA_BLADE) == ((place + offset) // STA_BLADE)
        term = jnp.einsum('ijs,vjs->vis', stiffness[d], shifted[:, :, d:d + STATIONS], precision=lax.Precision.HIGHEST)
        band = band + jnp.where(same[None, None, :], term, 0.0)
    beam_image = band - loads
    return flow_image, beam_image
```

```python
import functools

import jax
import jax.numpy as jnp
from jax import lax
from jax.experimental import pallas as pl
from jax.experimental.pallas import tpu as pltpu
from jax.sharding import PartitionSpec as P

F32 = jnp.float32
BF16 = jnp.bfloat16
LANES = 128
VMEM = pl.BlockSpec(memory_space=pltpu.VMEM)
LIMIT = 48 * 1024 * 1024


def params():
    return pltpu.CompilerParams(vmem_limit_bytes=LIMIT)


def halves(x):
    hi = x.astype(BF16).astype(F32)
    return jnp.concatenate([hi, x - hi], axis=0).astype(BF16)


def lane_row(x, width):
    return jnp.concatenate([x[r : r + 1, :width] for r in range(x.shape[0])], axis=1)


def table(stations, first, count):
    rows = lax.broadcasted_iota(jnp.int32, (count, stations.shape[1]), 0) + first
    return (rows == stations).astype(F32).astype(BF16)


def put_slabs(ref, base, rows):
    n = rows.shape[0]
    for h in range(rows.shape[1] // LANES):
        ref[base + h * n : base + (h + 1) * n] = rows[:, h * LANES : (h + 1) * LANES]


def get_slabs(ref, base, n, k):
    return jnp.concatenate([ref[base + h * n : base + (h + 1) * n] for h in range(k)], axis=1)


def relative(sta, me, sta_dev, ccols):
    return lane_row(sta[...] ^ (me * sta_dev), ccols)


def pre_kernel(span, flow, lmap, mask, sta, beam, p1, far, up, down, kept, wall):
    nvec, nvar, srows, ccols, _ = flow.shape
    ndof, _, sta_dev = beam.shape
    k = sta_dev // LANES
    rows = nvec * ndof
    halo = nvec * nvar * ccols
    me = lax.axis_index("span")
    near_row = jnp.where(me % 2 == 1, 0, srows - 1)
    far_row = srows - 1 - near_row
    lane = lax.broadcasted_iota(jnp.int32, (ccols, LANES), 1)
    packed = jnp.zeros((ccols, LANES), F32)
    for v in range(nvec):
        for b in range(nvar):
            q = v * nvar + b
            p1[q * ccols : (q + 1) * ccols] = flow[v, b, near_row]
            far[q * ccols : (q + 1) * ccols] = flow[v, b, far_row]
            up[q] = flow[v, b, :, ccols - 1, :]
            down[q] = flow[v, b, :, 0, :]
            for r in range(srows):
                at = q * 8 + r
                x = flow[v, b, r]
                if at:
                    x = pltpu.roll(x, at, 1)
                packed = jnp.where(lane == at, x, packed)
    surf = packed.T
    maskf = mask[...].astype(F32)
    for v in range(nvec):
        near = [surf[(v * nvar + a) * 8 : (v * nvar + a) * 8 + srows] * maskf for a in range(nvar)]
        for j in range(ndof):
            total = lmap[j, 0] * near[0]
            for a in range(1, nvar):
                total = total + lmap[j, a] * near[a]
            wall[v * ndof + j] = total
    walls = jnp.concatenate([wall[:, r, :] for r in range(srows)], axis=1)
    parts = halves(walls)
    stations = relative(sta, me, sta_dev, ccols)
    for p in range(span):
        both = lax.dot_general(
            parts,
            table(stations, p * sta_dev, sta_dev),
            (((1,), (1,)), ((), ())),
            preferred_element_type=F32,
        )
        term = both[:rows] + both[rows:]
        if p % 2:
            put_slabs(p1, halo + (p // 2) * rows * k, term)
        else:
            put_slabs(kept, (p // 2) * rows * k, term)
    base = halo + (span // 2) * rows * k
    for v in range(nvec):
        for j in range(ndof):
            for h in range(k):
                at = base + h * rows + v * ndof + j
                p1[at : at + 1] = beam[j, v : v + 1, h * LANES : (h + 1) * LANES]


def combine_kernel(halo, slab, sent, got, kept, own, *out):
    groups = len(out) + 1
    base = halo + groups * slab
    own[...] = kept[:slab] + got[halo : halo + slab]
    for q in range(1, groups):
        o = out[q - 1]
        o[:slab] = kept[q * slab : (q + 1) * slab] + got[halo + q * slab : halo + (q + 1) * slab]
        o[slab : 2 * slab] = sent[base : base + slab]
        o[2 * slab :] = got[base : base + slab]


def stencil_kernel(flow, jac, got, lo, hi, out, near):
    nvec, nvar, srows, ccols, _ = flow.shape
    r = pl.program_id(0)
    me = lax.axis_index("span")
    odd = me % 2
    row = lax.broadcasted_iota(jnp.int32, (ccols, LANES), 0)
    lane = lax.broadcasted_iota(jnp.int32, (ccols, LANES), 1)
    for v in range(nvec):
        for b in range(nvar):
            q = v * nvar + b
            x = flow[v, b, r]
            near[0, q] = jnp.where(row == 0, lo[q, pl.ds(r, 1)], pltpu.roll(x, 1, 0))
            near[1, q] = jnp.where(row == ccols - 1, hi[q, pl.ds(r, 1)], pltpu.roll(x, ccols - 1, 0))
            near[2, q] = jnp.where(lane == 0, 0.0, pltpu.roll(x, 1, 1))
            near[3, q] = jnp.where(lane == LANES - 1, 0.0, pltpu.roll(x, LANES - 1, 1))
    first, last = r == 0, r == srows - 1
    below = jnp.where(first, 0, r - 1)
    above = jnp.where(last, srows - 1, r + 1)
    low_on = jnp.where(odd == 1, 1.0, 0.0).astype(F32)
    high_on = 1.0 - low_on
    tile = 16

    def body(t, carry):
        c = pl.multiple_of(t * tile, tile)
        here = pl.ds(c, tile)
        acc = [[jnp.zeros((tile, LANES), F32) for _ in range(nvar)] for _ in range(nvec)]
        for e in range(7):
            for b in range(nvar):
                xs = []
                for v in range(nvec):
                    q = v * nvar + b
                    if e == 0:
                        x = flow[v, b, r, here]
                    elif e == 1:
                        h = got[pl.ds(q * ccols + c, tile)] * low_on
                        x = jnp.where(first, h, flow[v, b, below, here])
                    elif e == 2:
                        h = got[pl.ds(q * ccols + c, tile)] * high_on
                        x = jnp.where(last, h, flow[v, b, above, here])
                    else:
                        x = near[e - 3, q, here]
                    xs.append(x)
                for a in range(nvar):
                    m = jac[e, a, b, 0, here].astype(F32)
                    for v in range(nvec):
                        acc[v][a] = acc[v][a] + m * xs[v]
        for v in range(nvec):
            for a in range(nvar):
                out[v, a, 0, here] = acc[v][a]
        return carry

    lax.fori_loop(0, ccols // tile, body, 0)


def couple_kernel(
    span, flow_in, jac, far, motion, mask, sta, stiff, sent, got, *rest
):
    groups = span // 2
    zs = rest[: groups - 1]
    flow, band, gath, lk, block, sem = rest[groups - 1 :]
    nvec, nvar, srows, ccols, _ = flow_in.shape
    _, ndof, _, sta_dev = stiff.shape
    k = sta_dev // LANES
    rows = nvec * ndof
    slab = rows * k
    halo = nvec * nvar * ccols
    me = lax.axis_index("span")
    odd = me % 2
    e = 1 + odd
    r_far = jnp.where(odd == 1, srows - 1, 0)
    fetch = pltpu.make_async_copy(jac.at[e, :, :, r_far], block, sem)
    fetch.start()
    base = halo + groups * slab
    gath[0] = get_slabs(sent, base, rows, k)
    gath[1] = get_slabs(got, base, rows, k)
    for q in range(1, groups):
        gath[2 * q] = get_slabs(zs[q - 1], slab, rows, k)
        gath[2 * q + 1] = get_slabs(zs[q - 1], 2 * slab, rows, k)
    stations = relative(sta, me, sta_dev, ccols)
    both = jnp.zeros((2 * rows, srows * ccols), F32)
    for p in range(span):
        both = both + jnp.dot(
            halves(gath[p]), table(stations, p * sta_dev, sta_dev), preferred_element_type=F32
        )
    looked = both[:rows] + both[rows:]
    for r in range(srows):
        lk[:, r, :] = looked[:, r * ccols : (r + 1) * ccols]
    maskf = mask[...].astype(F32)
    tiles = []
    for v in range(nvec):
        for a in range(nvar):
            total = motion[a, 0] * lk[v * ndof]
            for j in range(1, ndof):
                total = total + motion[a, j] * lk[v * ndof + j]
            total = total * maskf
            tiles.append(jnp.concatenate([total, jnp.zeros((8 - srows, ccols), F32)], axis=0))
    tiles.append(jnp.zeros((LANES - 8 * len(tiles), ccols), F32))
    packed = jnp.concatenate(tiles, axis=0).T
    lane = lax.broadcasted_iota(jnp.int32, (ccols, LANES), 1)
    for v in range(nvec):
        for a in range(nvar):
            for r in range(srows):
                at = (v * nvar + a) * 8 + r
                x = packed if at == 0 else pltpu.roll(packed, LANES - at, 1)
                flow[v, a, r] = flow_in[v, a, r] + jnp.where(lane == 0, x, 0.0)
    own = gath[0]
    before = gath[jnp.where(me > 0, me ^ (me - 1), 0)]
    after = gath[jnp.where(me < span - 1, me ^ (me + 1), 0)]
    pos = lax.broadcasted_iota(jnp.int32, (rows, sta_dev), 1)
    place = pos + me * sta_dev
    stations_all = span * sta_dev
    blade_len = stations_all // 4

    def blade(t):
        n = jnp.zeros(t.shape, jnp.int32)
        for m in range(1, 5):
            n = n + (t + sta_dev // 2 >= m * blade_len).astype(jnp.int32)
        return n

    home = blade(place)
    shifted = []
    for d in range(5):
        s = d - 2
        other = place + s
        x = own if s == 0 else pltpu.roll(own, (-s) % sta_dev, 1)
        if s < 0:
            x = jnp.where(pos < -s, pltpu.roll(before, -s, 1), x)
        if s > 0:
            x = jnp.where(pos >= sta_dev - s, pltpu.roll(after, sta_dev - s, 1), x)
        good = (blade(other) == home) & (other >= 0) & (other < stations_all)
        x = jnp.where(good, x, 0.0)
        shifted.append([x[v * ndof : (v + 1) * ndof] for v in range(nvec)])
    for i in range(ndof):
        for v in range(nvec):
            total = stiff[0, i] * shifted[0][v]
            for d in range(1, 5):
                total = total + stiff[d, i] * shifted[d][v]
            band[i, v : v + 1, :] = jnp.sum(total, axis=0, keepdims=True)
    fetch.wait()
    tile = 16

    def body(t, carry):
        c = pl.multiple_of(t * tile, tile)
        here = pl.ds(c, tile)
        acc = [[flow[v, a, r_far, here] for a in range(nvar)] for v in range(nvec)]
        for b in range(nvar):
            xs = [far[pl.ds((v * nvar + b) * ccols + c, tile)] for v in range(nvec)]
            for a in range(nvar):
                m = block[a, b, here].astype(F32)
                for v in range(nvec):
                    acc[v][a] = acc[v][a] + m * xs[v]
        for v in range(nvec):
            for a in range(nvar):
                flow[v, a, r_far, here] = acc[v][a]
        return carry

    lax.fori_loop(0, ccols // tile, body, 0)


def last_kernel(band, *rest):
    parts, out = rest[:-1], rest[-1]
    ndof, nvec, sta_dev = band.shape
    rows = ndof * nvec
    total = parts[0][...]
    for p in parts[1:]:
        total = total + p[...]
    for v in range(nvec):
        for j in range(ndof):
            for h in range(sta_dev // LANES):
                at = h * rows + v * ndof + j
                cols = slice(h * LANES, (h + 1) * LANES)
                out[j, v : v + 1, cols] = band[j, v : v + 1, cols] - total[at : at + 1]


def reduce_kernel(own, *rest):
    parts, out = rest[:-1], rest[-1]
    total = own[...]
    for p in parts:
        total = total + p[: total.shape[0]]
    out[...] = total


def swap(x, axis, m):
    return lax.ppermute(x, axis, [(i, i ^ m) for i in range(lax.axis_size(axis))])


def on_device(
    flow_state, jacobians, beam_state, stiffness, motion_map, load_map, surface_mask, station_of
):
    nvec, nvar, srows, ccols, ncell = flow_state.shape
    ndof, sta_dev = beam_state.shape[1:]
    span, chord = lax.axis_size("span"), lax.axis_size("chord")
    groups = span // 2
    k = sta_dev // LANES
    rows = nvec * ndof
    slab = rows * k
    halo = nvec * nvar * ccols
    nq = nvec * nvar
    beam = jnp.transpose(beam_state, (1, 0, 2))

    def shape(*s):
        return jax.ShapeDtypeStruct(s, F32)

    p1, far, up, down, kept = pl.pallas_call(
        functools.partial(pre_kernel, span),
        out_shape=(
            shape(halo + (groups + 1) * slab, LANES),
            shape(halo, LANES),
            shape(nq, srows, LANES),
            shape(nq, srows, LANES),
            shape(groups * slab, LANES),
        ),
        in_specs=[VMEM] * 5,
        out_specs=(VMEM,) * 5,
        scratch_shapes=[pltpu.VMEM((rows, srows, ccols), F32)],
        compiler_params=params(),
        name="pre",
    )(flow_state, load_map, surface_mask, station_of, beam)

    pairs = []
    for i in range(1, span - 1, 2):
        pairs += [(i, i + 1), (i + 1, i)]
    far_got = lax.ppermute(far, "span", pairs)
    lo = lax.ppermute(up, "chord", [(i, i + 1) for i in range(chord - 1)])
    hi = lax.ppermute(down, "chord", [(i + 1, i) for i in range(chord - 1)])
    p1_got = swap(p1, "span", 1)

    own, *zs = pl.pallas_call(
        functools.partial(combine_kernel, halo, slab),
        out_shape=(shape(slab, LANES),) + (shape(3 * slab, LANES),) * (groups - 1),
        in_specs=[VMEM] * 3,
        out_specs=(VMEM,) * groups,
        compiler_params=params(),
        name="combine",
    )(p1, p1_got, kept)
    z_got = [swap(zs[q - 1], "span", 2 * q) for q in range(1, groups)]

    whole = pl.BlockSpec(flow_state.shape, lambda r: (0, 0, 0, 0, 0))
    flow1 = pl.pallas_call(
        stencil_kernel,
        grid=(srows,),
        out_shape=jax.ShapeDtypeStruct(flow_state.shape, F32),
        in_specs=[
            whole,
            pl.BlockSpec((7, nvar, nvar, 1, ccols, ncell), lambda r: (0, 0, 0, r, 0, 0)),
            pl.BlockSpec(p1_got.shape, lambda r: (0, 0)),
            pl.BlockSpec(lo.shape, lambda r: (0, 0, 0)),
            pl.BlockSpec(hi.shape, lambda r: (0, 0, 0)),
        ],
        out_specs=pl.BlockSpec((nvec, nvar, 1, ccols, ncell), lambda r: (0, 0, r, 0, 0)),
        scratch_shapes=[pltpu.VMEM((4, nq, ccols, LANES), F32)],
        compiler_params=params(),
        cost_estimate=pl.CostEstimate(
            flops=4 * 7 * nvar * nvar * srows * ccols * ncell,
            bytes_accessed=2 * jacobians.size + 8 * flow_state.size,
            transcendentals=0,
        ),
        name="stencil",
    )(flow_state, jacobians, p1_got, lo, hi)

    loads = pl.pallas_call(
        reduce_kernel,
        out_shape=shape(slab, LANES),
        in_specs=[VMEM] * groups,
        out_specs=VMEM,
        compiler_params=params(),
        name="reduce",
    )(own, *z_got)
    chord_got = [swap(loads, "chord", m) for m in range(1, chord)]

    flow_image, band = pl.pallas_call(
        functools.partial(couple_kernel, span),
        out_shape=(jax.ShapeDtypeStruct(flow_state.shape, F32), shape(ndof, nvec, sta_dev)),
        in_specs=[VMEM, pl.BlockSpec(memory_space=pl.ANY)] + [VMEM] * (7 + groups - 1),
        out_specs=(VMEM, VMEM),
        scratch_shapes=[
            pltpu.VMEM((span, rows, sta_dev), F32),
            pltpu.VMEM((rows, srows, ccols), F32),
            pltpu.VMEM((nvar, nvar, ccols, ncell), BF16),
            pltpu.SemaphoreType.DMA,
        ],
        compiler_params=params(),
        cost_estimate=pl.CostEstimate(flops=20000000, bytes_accessed=6000000, transcendentals=0),
        name="couple",
    )(
        flow1, jacobians, far_got, motion_map, surface_mask, station_of, stiffness, p1, p1_got, *z_got
    )

    out = pl.pallas_call(
        last_kernel,
        out_shape=shape(ndof, nvec, sta_dev),
        in_specs=[VMEM] * (chord + 1),
        out_specs=VMEM,
        compiler_params=params(),
        name="last",
    )(band, loads, *chord_got)
    return flow_image, jnp.transpose(out, (1, 0, 2))


def solution(mesh):
    in_specs = (
        P(None, None, "span", "chord", None),
        P(None, None, None, "span", "chord", None),
        P(None, None, "span"),
        P(None, None, None, "span"),
        P(None, None, "span", "chord"),
        P(None, None, "span", "chord"),
        P("span", "chord"),
        P("span", "chord"),
    )
    out_specs = (P(None, None, "span", "chord", None), P(None, None, "span"))
    return jax.shard_map(
        on_device, mesh=mesh, in_specs=in_specs, out_specs=out_specs, check_vma=False
    )
```

```python
import functools

import jax
import jax.numpy as jnp
from jax import lax
from jax.experimental import pallas as pl
from jax.experimental.pallas import tpu as pltpu
from jax.sharding import PartitionSpec as P

F32 = jnp.float32
BF16 = jnp.bfloat16
LANES = 128
VMEM = pl.BlockSpec(memory_space=pltpu.VMEM)
LIMIT = 16 * 1024 * 1024
FIRST = 20000000000


def params():
    return pltpu.CompilerParams(vmem_limit_bytes=LIMIT)


def halves(x):
    hi = x.astype(BF16).astype(F32)
    return jnp.concatenate([hi, x - hi], axis=0).astype(BF16)


def lane_row(x, width):
    return jnp.concatenate([x[r : r + 1, :width] for r in range(x.shape[0])], axis=1)


def table(stations, first, count):
    rows = lax.broadcasted_iota(jnp.int32, (count, stations.shape[1]), 0) + first
    return (rows == stations).astype(F32).astype(BF16)


def put_slabs(ref, base, rows):
    n = rows.shape[0]
    for h in range(rows.shape[1] // LANES):
        ref[base + h * n : base + (h + 1) * n] = rows[:, h * LANES : (h + 1) * LANES]


def get_slabs(ref, base, n, k):
    return jnp.concatenate([ref[base + h * n : base + (h + 1) * n] for h in range(k)], axis=1)


def relative(sta, me, sta_dev, ccols):
    return lane_row(sta[...] ^ (me * sta_dev), ccols)


def face_kernel(flow, near, far, beside, across, surf):
    nvec, nvar, srows, ccols, _ = flow.shape
    odd = lax.axis_index("span") % 2 == 1
    near_row = jnp.where(odd, 0, srows - 1)
    far_row = srows - 1 - near_row
    codd = lax.axis_index("chord") % 2 == 1
    near_col = jnp.where(codd, 0, 1)
    lane = lax.broadcasted_iota(jnp.int32, (ccols, LANES), 1)
    packed = jnp.zeros((ccols, LANES), F32)
    for v in range(nvec):
        for b in range(nvar):
            q = v * nvar + b
            near[q * ccols : (q + 1) * ccols] = flow[v, b, near_row]
            far[q * ccols : (q + 1) * ccols] = flow[v, b, far_row]
            low, high = flow[v, b, :, 0, :], flow[v, b, :, ccols - 1, :]
            beside[q] = jnp.where(near_col == 0, low, high)
            across[q] = jnp.where(near_col == 0, high, low)
            for r in range(srows):
                at = q * 8 + r
                x = flow[v, b, r]
                if at:
                    x = pltpu.roll(x, at, 1)
                packed = jnp.where(lane == at, x, packed)
    surf[...] = packed.T


def pre_kernel(span, surf_in, lmap, mask, sta, beam, p1, kept, rel, maskf_out, wall):
    nvar = lmap.shape[1]
    srows, ccols = mask.shape
    ndof, nvec, sta_dev = beam.shape
    k = sta_dev // LANES
    rows = nvec * ndof
    me = lax.axis_index("span")
    surf = surf_in[...]
    maskf = mask[...].astype(F32)
    maskf_out[...] = maskf
    for v in range(nvec):
        near = [surf[(v * nvar + a) * 8 : (v * nvar + a) * 8 + srows] * maskf for a in range(nvar)]
        for j in range(ndof):
            total = lmap[j, 0] * near[0]
            for a in range(1, nvar):
                total = total + lmap[j, a] * near[a]
            wall[v * ndof + j] = total
    walls = jnp.concatenate([wall[:, r, :] for r in range(srows)], axis=1)
    parts = halves(walls)
    stations = relative(sta, me, sta_dev, ccols)
    rel[...] = stations
    for p in range(span):
        both = lax.dot_general(
            parts,
            table(stations, p * sta_dev, sta_dev),
            (((1,), (1,)), ((), ())),
            preferred_element_type=F32,
        )
        put_slabs(p1 if p % 2 else kept, (p // 2) * rows * k, both[:rows] + both[rows:])
    base = (span // 2) * rows * k
    for v in range(nvec):
        for j in range(ndof):
            for h in range(k):
                at = base + h * rows + v * ndof + j
                p1[at : at + 1] = beam[j, v : v + 1, h * LANES : (h + 1) * LANES]


def combine_kernel(slab, sent, got, kept, own, *out):
    groups = len(out) + 1
    base = groups * slab
    own[...] = kept[:slab] + got[:slab]
    for q in range(1, groups):
        o = out[q - 1]
        o[:slab] = kept[q * slab : (q + 1) * slab] + got[q * slab : (q + 1) * slab]
        o[slab : 2 * slab] = sent[base : base + slab]
        o[2 * slab :] = got[base : base + slab]


def stencil_kernel(chord, flow, jac, got, beside, across, out, near):
    nvec, nvar, srows, ccols, _ = flow.shape
    me = lax.axis_index("span")
    odd = me % 2
    row = lax.broadcasted_iota(jnp.int32, (ccols, LANES), 0)
    lane = lax.broadcasted_iota(jnp.int32, (ccols, LANES), 1)
    low_on = jnp.where(odd == 1, 1.0, 0.0).astype(F32)
    high_on = 1.0 - low_on
    column = lax.axis_index("chord")
    codd = column % 2
    inner = jnp.where((column > 0) & (column < chord - 1), 1.0, 0.0).astype(F32)
    tile = 16

    def one_row(r, carry):
        for v in range(nvec):
            for b in range(nvar):
                q = v * nvar + b
                x = flow[v, b, r]
                left, right = pltpu.roll(x, 1, 0), pltpu.roll(x, ccols - 1, 0)
                one, two = beside[q, pl.ds(r, 1)], across[q, pl.ds(r, 1)] * inner
                near[0, q] = jnp.where(row == 0, jnp.where(codd == 1, one, two), left)
                near[1, q] = jnp.where(row == ccols - 1, jnp.where(codd == 1, two, one), right)
                near[2, q] = jnp.where(lane == 0, 0.0, pltpu.roll(x, 1, 1))
                near[3, q] = jnp.where(lane == LANES - 1, 0.0, pltpu.roll(x, LANES - 1, 1))
        first, last = r == 0, r == srows - 1
        below = jnp.where(first, 0, r - 1)
        above = jnp.where(last, srows - 1, r + 1)

        def one_tile(t, carry):
            c = pl.multiple_of(t * tile, tile)
            here = pl.ds(c, tile)
            acc = [[jnp.zeros((tile, LANES), F32) for _ in range(nvar)] for _ in range(nvec)]
            for e in range(7):
                for b in range(nvar):
                    xs = []
                    for v in range(nvec):
                        q = v * nvar + b
                        if e == 0:
                            x = flow[v, b, r, here]
                        elif e == 1:
                            h = got[pl.ds(q * ccols + c, tile)] * low_on
                            x = jnp.where(first, h, flow[v, b, below, here])
                        elif e == 2:
                            h = got[pl.ds(q * ccols + c, tile)] * high_on
                            x = jnp.where(last, h, flow[v, b, above, here])
                        else:
                            x = near[e - 3, q, here]
                        xs.append(x)
                    for a in range(nvar):
                        m = jac[e, a, b, r, here].astype(F32)
                        for v in range(nvec):
                            acc[v][a] = acc[v][a] + m * xs[v]
            for v in range(nvec):
                for a in range(nvar):
                    out[v, a, r, here] = acc[v][a]
            return carry

        return lax.fori_loop(0, ccols // tile, one_tile, carry)

    lax.fori_loop(0, srows, one_row, 0)


def couple_kernel(
    span, flow_in, jac, far, motion, mask, rel, stiff, sent, got, *rest
):
    groups = span // 2
    zs = rest[: groups - 1]
    flow, band, gath, lk = rest[groups - 1 :]
    nvec, nvar, srows, ccols, _ = flow_in.shape
    _, ndof, _, sta_dev = stiff.shape
    k = sta_dev // LANES
    rows = nvec * ndof
    slab = rows * k
    me = lax.axis_index("span")
    odd = me % 2
    e = 1 + odd
    inner = jnp.where((me > 0) & (me < span - 1), 1.0, 0.0).astype(F32)
    r_far = jnp.where(odd == 1, srows - 1, 0)
    base = groups * slab
    gath[0] = get_slabs(sent, base, rows, k)
    gath[1] = get_slabs(got, base, rows, k)
    for q in range(1, groups):
        gath[2 * q] = get_slabs(zs[q - 1], slab, rows, k)
        gath[2 * q + 1] = get_slabs(zs[q - 1], 2 * slab, rows, k)
    stations = rel[...]
    both = jnp.zeros((2 * rows, srows * ccols), F32)
    for p in range(span):
        both = both + jnp.dot(
            halves(gath[p]), table(stations, p * sta_dev, sta_dev), preferred_element_type=F32
        )
    looked = both[:rows] + both[rows:]
    for r in range(srows):
        lk[:, r, :] = looked[:, r * ccols : (r + 1) * ccols]
    maskf = mask[...]
    tiles = []
    for v in range(nvec):
        for a in range(nvar):
            total = motion[a, 0] * lk[v * ndof]
            for j in range(1, ndof):
                total = total + motion[a, j] * lk[v * ndof + j]
            total = total * maskf
            tiles.append(jnp.concatenate([total, jnp.zeros((8 - srows, ccols), F32)], axis=0))
    tiles.append(jnp.zeros((LANES - 8 * len(tiles), ccols), F32))
    packed = jnp.concatenate(tiles, axis=0).T
    lane = lax.broadcasted_iota(jnp.int32, (ccols, LANES), 1)
    for v in range(nvec):
        for a in range(nvar):
            for r in range(srows):
                at = (v * nvar + a) * 8 + r
                x = packed if at == 0 else pltpu.roll(packed, LANES - at, 1)
                flow[v, a, r] = flow_in[v, a, r] + jnp.where(lane == 0, x, 0.0)
    own = gath[0]
    before = gath[jnp.where(me > 0, me ^ (me - 1), 0)]
    after = gath[jnp.where(me < span - 1, me ^ (me + 1), 0)]
    pos = lax.broadcasted_iota(jnp.int32, (rows, sta_dev), 1)
    place = pos + me * sta_dev
    stations_all = span * sta_dev
    blade_len = stations_all // 4

    def blade(t):
        n = jnp.zeros(t.shape, jnp.int32)
        for m in range(1, 5):
            n = n + (t + sta_dev // 2 >= m * blade_len).astype(jnp.int32)
        return n

    home = blade(place)
    shifted = []
    for d in range(5):
        s = d - 2
        other = place + s
        x = own if s == 0 else pltpu.roll(own, (-s) % sta_dev, 1)
        if s < 0:
            x = jnp.where(pos < -s, pltpu.roll(before, -s, 1), x)
        if s > 0:
            x = jnp.where(pos >= sta_dev - s, pltpu.roll(after, sta_dev - s, 1), x)
        good = (blade(other) == home) & (other >= 0) & (other < stations_all)
        x = jnp.where(good, x, 0.0)
        shifted.append([x[v * ndof : (v + 1) * ndof] for v in range(nvec)])
    for i in range(ndof):
        for v in range(nvec):
            total = stiff[0, i] * shifted[0][v]
            for d in range(1, 5):
                total = total + stiff[d, i] * shifted[d][v]
            band[i, v : v + 1, :] = jnp.sum(total, axis=0, keepdims=True)
    tile = 16

    def body(t, carry):
        c = pl.multiple_of(t * tile, tile)
        here = pl.ds(c, tile)
        acc = [[flow[v, a, r_far, here] for a in range(nvar)] for v in range(nvec)]
        for b in range(nvar):
            xs = [far[pl.ds((v * nvar + b) * ccols + c, tile)] * inner for v in range(nvec)]
            for a in range(nvar):
                m = jac[e, a, b, r_far, here].astype(F32)
                for v in range(nvec):
                    acc[v][a] = acc[v][a] + m * xs[v]
        for v in range(nvec):
            for a in range(nvar):
                flow[v, a, r_far, here] = acc[v][a]
        return carry

    lax.fori_loop(0, ccols // tile, body, 0)


def last_kernel(band, *rest):
    parts, out = rest[:-1], rest[-1]
    ndof, nvec, sta_dev = band.shape
    rows = ndof * nvec
    total = parts[0][...]
    for p in parts[1:]:
        total = total + p[...]
    for v in range(nvec):
        for j in range(ndof):
            for h in range(sta_dev // LANES):
                at = h * rows + v * ndof + j
                cols = slice(h * LANES, (h + 1) * LANES)
                out[j, v : v + 1, cols] = band[j, v : v + 1, cols] - total[at : at + 1]


def reduce_kernel(_, own, *rest):
    parts, out = rest[:-1], rest[-1]
    total = own[...]
    for p in parts:
        total = total + p[: total.shape[0]]
    out[...] = total


def swap(x, axis, m):
    return lax.ppermute(x, axis, [(i, i ^ m) for i in range(lax.axis_size(axis))])


def others(span, chord, along_span):
    pairs = []
    for i in range(span):
        for c in range(chord):
            at, size = (i, span) if along_span else (c, chord)
            if 0 < at < size - 1:
                to = at + 1 if at % 2 else at - 1
                to = (to, c) if along_span else (i, to)
            else:
                to = (i, c ^ 1) if along_span else (i ^ 1, c)
            pairs.append((i * chord + c, to[0] * chord + to[1]))
    return pairs


def on_device(
    flow_state, jacobians, beam_state, stiffness, motion_map, load_map, surface_mask, station_of
):
    nvec, nvar, srows, ccols, ncell = flow_state.shape
    ndof, sta_dev = beam_state.shape[1:]
    span, chord = lax.axis_size("span"), lax.axis_size("chord")
    groups = span // 2
    k = sta_dev // LANES
    rows = nvec * ndof
    slab = rows * k
    halo = nvec * nvar * ccols
    nq = nvec * nvar
    beam = jnp.transpose(beam_state, (1, 0, 2))

    def shape(*s):
        return jax.ShapeDtypeStruct(s, F32)

    near, far, beside, across, surf = pl.pallas_call(
        face_kernel,
        out_shape=(
            shape(halo, LANES),
            shape(halo, LANES),
            shape(nq, srows, LANES),
            shape(nq, srows, LANES),
            shape(LANES, ccols),
        ),
        in_specs=[VMEM],
        out_specs=(VMEM,) * 5,
        compiler_params=params(),
        cost_estimate=pl.CostEstimate(flops=FIRST, bytes_accessed=2000000, transcendentals=0),
        name="faces",
    )(flow_state)
    far_got = lax.ppermute(far, ("span", "chord"), others(span, chord, True))
    beside_got = swap(beside, "chord", 1)
    across_got = lax.ppermute(across, ("span", "chord"), others(span, chord, False))
    near_got = swap(near, "span", 1)

    p1, kept, rel, maskf = pl.pallas_call(
        functools.partial(pre_kernel, span),
        out_shape=(
            shape((groups + 1) * slab, LANES),
            shape(groups * slab, LANES),
            jax.ShapeDtypeStruct((1, srows * ccols), jnp.int32),
            shape(srows, ccols),
        ),
        in_specs=[VMEM] * 5,
        out_specs=(VMEM,) * 4,
        scratch_shapes=[pltpu.VMEM((rows, srows, ccols), F32)],
        compiler_params=params(),
        cost_estimate=pl.CostEstimate(flops=FIRST, bytes_accessed=1000000, transcendentals=0),
        name="pre",
    )(surf, load_map, surface_mask, station_of, beam)
    p1_got = swap(p1, "span", 1)

    own, *zs = pl.pallas_call(
        functools.partial(combine_kernel, slab),
        out_shape=(shape(slab, LANES),) + (shape(3 * slab, LANES),) * (groups - 1),
        in_specs=[VMEM] * 3,
        out_specs=(VMEM,) * groups,
        compiler_params=params(),
        name="combine",
    )(p1, p1_got, kept)
    z_got = [swap(zs[q - 1], "span", 2 * q) for q in range(1, groups)]

    flow1 = pl.pallas_call(
        functools.partial(stencil_kernel, chord),
        out_shape=jax.ShapeDtypeStruct(flow_state.shape, F32),
        in_specs=[VMEM] * 5,
        out_specs=VMEM,
        scratch_shapes=[pltpu.VMEM((4, nq, ccols, LANES), F32)],
        compiler_params=params(),
        cost_estimate=pl.CostEstimate(
            flops=4 * 7 * nvar * nvar * srows * ccols * ncell,
            bytes_accessed=2 * jacobians.size + 8 * flow_state.size,
            transcendentals=0,
        ),
        name="stencil",
    )(flow_state, jacobians, near_got, beside_got, across_got)

    loads = pl.pallas_call(
        reduce_kernel,
        out_shape=shape(slab, LANES),
        in_specs=[pl.BlockSpec(memory_space=pl.ANY)] + [VMEM] * groups,
        out_specs=VMEM,
        compiler_params=params(),
        name="reduce",
    )(flow1, own, *z_got)
    chord_got = [swap(loads, "chord", m) for m in range(1, chord)]

    flow_image, band = pl.pallas_call(
        functools.partial(couple_kernel, span),
        out_shape=(jax.ShapeDtypeStruct(flow_state.shape, F32), shape(ndof, nvec, sta_dev)),
        in_specs=[VMEM] * (9 + groups - 1),
        out_specs=(VMEM, VMEM),
        scratch_shapes=[
            pltpu.VMEM((span, rows, sta_dev), F32),
            pltpu.VMEM((rows, srows, ccols), F32),
        ],
        compiler_params=params(),
        cost_estimate=pl.CostEstimate(flops=20000000, bytes_accessed=6000000, transcendentals=0),
        name="couple",
    )(
        flow1, jacobians, far_got, motion_map, maskf, rel, stiffness, p1, p1_got, *z_got
    )

    out = pl.pallas_call(
        last_kernel,
        out_shape=shape(ndof, nvec, sta_dev),
        in_specs=[VMEM] * (chord + 1),
        out_specs=VMEM,
        compiler_params=params(),
        name="last",
    )(band, loads, *chord_got)
    return flow_image, jnp.transpose(out, (1, 0, 2))


def solution(mesh):
    in_specs = (
        P(None, None, "span", "chord", None),
        P(None, None, None, "span", "chord", None),
        P(None, None, "span"),
        P(None, None, None, "span"),
        P(None, None, "span", "chord"),
        P(None, None, "span", "chord"),
        P("span", "chord"),
        P("span", "chord"),
    )
    out_specs = (P(None, None, "span", "chord", None), P(None, None, "span"))
    return jax.shard_map(
        on_device, mesh=mesh, in_specs=in_specs, out_specs=out_specs, check_vma=False
    )
```

```python
import functools

import jax
import jax.numpy as jnp
from jax import lax
from jax.experimental import pallas as pl
from jax.experimental.pallas import tpu as pltpu
from jax.sharding import PartitionSpec as P

F32 = jnp.float32
BF16 = jnp.bfloat16
LANES = 128
VMEM = pl.BlockSpec(memory_space=pltpu.VMEM)
LIMIT = 16 * 1024 * 1024
FIRST = 20000000000


def params():
    return pltpu.CompilerParams(vmem_limit_bytes=LIMIT)


def halves(x):
    hi = x.astype(BF16).astype(F32)
    return jnp.concatenate([hi, x - hi], axis=0).astype(BF16)


def lane_row(x, width):
    return jnp.concatenate([x[r : r + 1, :width] for r in range(x.shape[0])], axis=1)


def table(stations, first, count):
    rows = lax.broadcasted_iota(jnp.int32, (count, stations.shape[1]), 0) + first
    return (rows == stations).astype(F32).astype(BF16)


def put_slabs(ref, base, rows):
    n = rows.shape[0]
    for h in range(rows.shape[1] // LANES):
        ref[base + h * n : base + (h + 1) * n] = rows[:, h * LANES : (h + 1) * LANES]


def get_slabs(ref, base, n, k):
    return jnp.concatenate([ref[base + h * n : base + (h + 1) * n] for h in range(k)], axis=1)


def relative(sta, me, sta_dev, ccols):
    return lane_row(sta[...] ^ (me * sta_dev), ccols)


def face_kernel(flow, near, far, low, high, surf):
    nvec, nvar, srows, ccols, _ = flow.shape
    odd = lax.axis_index("span") % 2 == 1
    near_row = jnp.where(odd, 0, srows - 1)
    far_row = srows - 1 - near_row
    lane = lax.broadcasted_iota(jnp.int32, (ccols, LANES), 1)
    packed = jnp.zeros((ccols, LANES), F32)
    for v in range(nvec):
        for b in range(nvar):
            q = v * nvar + b
            near[q * ccols : (q + 1) * ccols] = flow[v, b, near_row]
            far[q * ccols : (q + 1) * ccols] = flow[v, b, far_row]
            low[q * srows : (q + 1) * srows] = flow[v, b, :, 0, :]
            high[q * srows : (q + 1) * srows] = flow[v, b, :, ccols - 1, :]
            for r in range(srows):
                at = q * 8 + r
                x = flow[v, b, r]
                if at:
                    x = pltpu.roll(x, at, 1)
                packed = jnp.where(lane == at, x, packed)
    surf[...] = packed.T


def neighbour_steps(chord):
    return [m for m in range(1, chord) if m & (m + 1) == 0]


def wall_kernel(chord, sta_dev, surf_in, lmap, mask, sta, low, high, *refs):
    messages, (rel, maskf_out, wall) = refs[: chord - 1], refs[chord - 1 :]
    rows = wall.shape[0]
    nvar = lmap.shape[1]
    ndof = lmap.shape[0]
    nvec = rows // ndof
    srows, ccols = mask.shape
    slab = rows * (srows * ccols // LANES)
    me = lax.axis_index("span")
    column = lax.axis_index("chord")
    surf = surf_in[...]
    maskf = mask[...].astype(F32)
    maskf_out[...] = maskf
    for v in range(nvec):
        near = [surf[(v * nvar + a) * 8 : (v * nvar + a) * 8 + srows] * maskf for a in range(nvar)]
        for j in range(ndof):
            total = lmap[j, 0] * near[0]
            for a in range(1, nvar):
                total = total + lmap[j, a] * near[a]
            wall[v * ndof + j] = total
    walls = jnp.concatenate([wall[:, r, :] for r in range(srows)], axis=1)
    stations = relative(sta, me, sta_dev, ccols)
    rel[...] = stations
    numbers = jnp.broadcast_to(stations.astype(F32), (8, stations.shape[1]))
    for m in range(1, chord):
        message = messages[m - 1]
        put_slabs(message, 0, walls)
        put_slabs(message, slab, numbers)
        if m in neighbour_steps(chord):
            base = slab + 8 * (walls.shape[1] // LANES)
            message[base:] = jnp.where((column ^ m) > column, high[...], low[...])


def dense_terms(span, first, rel, walls, rows, sta_dev, out):
    wide = rel.shape[1] // LANES
    k = sta_dev // LANES
    slab = rows * wide
    parts = [halves(get_slabs(x, 0, rows, wide)) for x in walls]
    stations = [rel[...]]
    for x in walls[1:]:
        stations.append(get_slabs(x, slab, 8, wide)[:1].astype(jnp.int32))
    for p in range(first, span, 2):
        both = 0.0
        for x, st in zip(parts, stations):
            both = both + lax.dot_general(
                x,
                table(st, p * sta_dev, sta_dev),
                (((1,), (1,)), ((), ())),
                preferred_element_type=F32,
            )
        put_slabs(out, (p // 2) * rows * k, both[:rows] + both[rows:])


def send_kernel(span, chord, rel, beam, *refs):
    walls, (p1, lo, hi) = refs[:chord], refs[chord:]
    ndof, nvec, sta_dev = beam.shape
    k = sta_dev // LANES
    rows = nvec * ndof
    column = lax.axis_index("chord")
    dense_terms(span, 1, rel, walls, rows, sta_dev, p1)
    at0 = (span // 2) * rows * k
    for v in range(nvec):
        for j in range(ndof):
            for h in range(k):
                at = at0 + h * rows + v * ndof + j
                p1[at : at + 1] = beam[j, v : v + 1, h * LANES : (h + 1) * LANES]
    base = (rows + 8) * (rel.shape[1] // LANES)
    low, high = jnp.zeros(lo.shape, F32), jnp.zeros(hi.shape, F32)
    for m in neighbour_steps(chord):
        x = walls[m][base:]
        low = jnp.where((column > 0) & ((column ^ (column - 1)) == m), x, low)
        high = jnp.where((column < chord - 1) & ((column ^ (column + 1)) == m), x, high)
    lo[...] = low
    hi[...] = high


def keep_kernel(span, chord, rows, sta_dev, rel, *refs):
    walls, kept = refs[:chord], refs[-1]
    dense_terms(span, 0, rel, walls, rows, sta_dev, kept)


def combine_kernel(slab, sent, got, kept, own, *out):
    groups = len(out) + 1
    base = groups * slab
    own[...] = kept[:slab] + got[:slab]
    for q in range(1, groups):
        o = out[q - 1]
        o[:slab] = kept[q * slab : (q + 1) * slab] + got[q * slab : (q + 1) * slab]
        o[slab : 2 * slab] = sent[base : base + slab]
        o[2 * slab :] = got[base : base + slab]


def stencil_kernel(span, flow, jac, got, far, lo, hi, _, out, near, faces):
    nvec, nvar, srows, ccols, _ = flow.shape
    me = lax.axis_index("span")
    odd = me % 2
    row = lax.broadcasted_iota(jnp.int32, (ccols, LANES), 0)
    lane = lax.broadcasted_iota(jnp.int32, (ccols, LANES), 1)
    inner = jnp.where((me > 0) & (me < span - 1), 1.0, 0.0).astype(F32)
    tile = 16
    for q in range(nvec * nvar):
        one, two = got[q * ccols : (q + 1) * ccols], far[q * ccols : (q + 1) * ccols] * inner
        faces[0, q] = jnp.where(odd == 1, one, two)
        faces[1, q] = jnp.where(odd == 1, two, one)

    def one_row(r, carry):
        for v in range(nvec):
            for b in range(nvar):
                q = v * nvar + b
                x = flow[v, b, r]
                left, right = pltpu.roll(x, 1, 0), pltpu.roll(x, ccols - 1, 0)
                near[0, q] = jnp.where(row == 0, lo[pl.ds(q * srows + r, 1)], left)
                near[1, q] = jnp.where(row == ccols - 1, hi[pl.ds(q * srows + r, 1)], right)
                near[2, q] = jnp.where(lane == 0, 0.0, pltpu.roll(x, 1, 1))
                near[3, q] = jnp.where(lane == LANES - 1, 0.0, pltpu.roll(x, LANES - 1, 1))
        first, last = r == 0, r == srows - 1
        below = jnp.where(first, 0, r - 1)
        above = jnp.where(last, srows - 1, r + 1)

        def one_tile(t, carry):
            c = pl.multiple_of(t * tile, tile)
            here = pl.ds(c, tile)
            acc = [[jnp.zeros((tile, LANES), F32) for _ in range(nvar)] for _ in range(nvec)]
            for e in range(7):
                for b in range(nvar):
                    xs = []
                    for v in range(nvec):
                        q = v * nvar + b
                        if e == 0:
                            x = flow[v, b, r, here]
                        elif e == 1:
                            x = jnp.where(first, faces[0, q, here], flow[v, b, below, here])
                        elif e == 2:
                            x = jnp.where(last, faces[1, q, here], flow[v, b, above, here])
                        else:
                            x = near[e - 3, q, here]
                        xs.append(x)
                    for a in range(nvar):
                        m = jac[e, a, b, r, here].astype(F32)
                        for v in range(nvec):
                            acc[v][a] = acc[v][a] + m * xs[v]
            for v in range(nvec):
                for a in range(nvar):
                    out[v, a, r, here] = acc[v][a]
            return carry

        return lax.fori_loop(0, ccols // tile, one_tile, carry)

    lax.fori_loop(0, srows, one_row, 0)


def couple_kernel(
    span, flow_in, motion, mask, rel, stiff, sent, got, own_loads, *rest
):
    groups = span // 2
    zs = rest[: groups - 1]
    flow, beam_out, gath, lk = rest[groups - 1 :]
    nvec, nvar, srows, ccols, _ = flow_in.shape
    _, ndof, _, sta_dev = stiff.shape
    k = sta_dev // LANES
    rows = nvec * ndof
    slab = rows * k
    me = lax.axis_index("span")
    base = groups * slab
    gath[0] = get_slabs(sent, base, rows, k)
    gath[1] = get_slabs(got, base, rows, k)
    for q in range(1, groups):
        gath[2 * q] = get_slabs(zs[q - 1], slab, rows, k)
        gath[2 * q + 1] = get_slabs(zs[q - 1], 2 * slab, rows, k)
    stations = rel[...]
    both = jnp.zeros((2 * rows, srows * ccols), F32)
    for p in range(span):
        both = both + jnp.dot(
            halves(gath[p]), table(stations, p * sta_dev, sta_dev), preferred_element_type=F32
        )
    looked = both[:rows] + both[rows:]
    for r in range(srows):
        lk[:, r, :] = looked[:, r * ccols : (r + 1) * ccols]
    maskf = mask[...]
    tiles = []
    for v in range(nvec):
        for a in range(nvar):
            total = motion[a, 0] * lk[v * ndof]
            for j in range(1, ndof):
                total = total + motion[a, j] * lk[v * ndof + j]
            total = total * maskf
            tiles.append(jnp.concatenate([total, jnp.zeros((8 - srows, ccols), F32)], axis=0))
    tiles.append(jnp.zeros((LANES - 8 * len(tiles), ccols), F32))
    packed = jnp.concatenate(tiles, axis=0).T
    lane = lax.broadcasted_iota(jnp.int32, (ccols, LANES), 1)
    for v in range(nvec):
        for a in range(nvar):
            for r in range(srows):
                at = (v * nvar + a) * 8 + r
                x = packed if at == 0 else pltpu.roll(packed, LANES - at, 1)
                flow[v, a, r] = flow_in[v, a, r] + jnp.where(lane == 0, x, 0.0)
    own = gath[0]
    before = gath[jnp.where(me > 0, me ^ (me - 1), 0)]
    after = gath[jnp.where(me < span - 1, me ^ (me + 1), 0)]
    pos = lax.broadcasted_iota(jnp.int32, (rows, sta_dev), 1)
    place = pos + me * sta_dev
    stations_all = span * sta_dev
    blade_len = stations_all // 4

    def blade(t):
        n = jnp.zeros(t.shape, jnp.int32)
        for m in range(1, 5):
            n = n + (t + sta_dev // 2 >= m * blade_len).astype(jnp.int32)
        return n

    home = blade(place)
    shifted = []
    for d in range(5):
        s = d - 2
        other = place + s
        x = own if s == 0 else pltpu.roll(own, (-s) % sta_dev, 1)
        if s < 0:
            x = jnp.where(pos < -s, pltpu.roll(before, -s, 1), x)
        if s > 0:
            x = jnp.where(pos >= sta_dev - s, pltpu.roll(after, sta_dev - s, 1), x)
        good = (blade(other) == home) & (other >= 0) & (other < stations_all)
        x = jnp.where(good, x, 0.0)
        shifted.append([x[v * ndof : (v + 1) * ndof] for v in range(nvec)])
    loads = own_loads[...]
    for z in zs:
        loads = loads + z[:slab]
    loads = jnp.concatenate([loads[h * rows : (h + 1) * rows] for h in range(k)], axis=1)
    for i in range(ndof):
        for v in range(nvec):
            total = stiff[0, i] * shifted[0][v]
            for d in range(1, 5):
                total = total + stiff[d, i] * shifted[d][v]
            at = v * ndof + i
            beam_out[i, v : v + 1, :] = jnp.sum(total, axis=0, keepdims=True) - loads[at : at + 1]


def swap(x, axis, m):
    return lax.ppermute(x, axis, [(i, i ^ m) for i in range(lax.axis_size(axis))])


def far_pairs(span, chord):
    pairs = []
    for i in range(span):
        for c in range(chord):
            if 0 < i < span - 1:
                to = (i + 1 if i % 2 else i - 1, c)
            else:
                to = (i, c ^ 1)
            pairs.append((i * chord + c, to[0] * chord + to[1]))
    return pairs


def on_device(
    flow_state, jacobians, beam_state, stiffness, motion_map, load_map, surface_mask, station_of
):
    nvec, nvar, srows, ccols, ncell = flow_state.shape
    ndof, sta_dev = beam_state.shape[1:]
    span, chord = lax.axis_size("span"), lax.axis_size("chord")
    groups = span // 2
    k = sta_dev // LANES
    rows = nvec * ndof
    slab = rows * k
    halo = nvec * nvar * ccols
    nq = nvec * nvar
    beam = jnp.transpose(beam_state, (1, 0, 2))

    def shape(*s):
        return jax.ShapeDtypeStruct(s, F32)

    near, far, low, high, surf = pl.pallas_call(
        face_kernel,
        out_shape=(
            shape(halo, LANES),
            shape(halo, LANES),
            shape(nq * srows, LANES),
            shape(nq * srows, LANES),
            shape(LANES, ccols),
        ),
        in_specs=[VMEM],
        out_specs=(VMEM,) * 5,
        compiler_params=params(),
        cost_estimate=pl.CostEstimate(flops=FIRST, bytes_accessed=2000000, transcendentals=0),
        name="faces",
    )(flow_state)
    near_got = swap(near, "span", 1)
    far_got = lax.ppermute(far, ("span", "chord"), far_pairs(span, chord))

    wide = srows * ccols // LANES
    wall_rows = (rows + 8) * wide
    message_rows = [
        wall_rows + (nq * srows if m in neighbour_steps(chord) else 0) for m in range(1, chord)
    ]
    *messages, rel, maskf = pl.pallas_call(
        functools.partial(wall_kernel, chord, sta_dev),
        out_shape=tuple(shape(n, LANES) for n in message_rows)
        + (jax.ShapeDtypeStruct((1, srows * ccols), jnp.int32), shape(srows, ccols)),
        in_specs=[VMEM] * 6,
        out_specs=(VMEM,) * (chord + 1),
        scratch_shapes=[pltpu.VMEM((rows, srows, ccols), F32)],
        compiler_params=params(),
        cost_estimate=pl.CostEstimate(flops=FIRST, bytes_accessed=1000000, transcendentals=0),
        name="wall",
    )(surf, load_map, surface_mask, station_of, low, high)
    wall_got = [swap(messages[m - 1], "chord", m) for m in range(1, chord)]

    p1, lo, hi = pl.pallas_call(
        functools.partial(send_kernel, span, chord),
        out_shape=(
            shape((groups + 1) * slab, LANES),
            shape(nq * srows, LANES),
            shape(nq * srows, LANES),
        ),
        in_specs=[VMEM] * (chord + 2),
        out_specs=(VMEM,) * 3,
        compiler_params=params(),
        cost_estimate=pl.CostEstimate(flops=FIRST, bytes_accessed=1000000, transcendentals=0),
        name="send",
    )(rel, beam, messages[0], *wall_got)
    p1_got = swap(p1, "span", 1)
    kept = pl.pallas_call(
        functools.partial(keep_kernel, span, chord, rows, sta_dev),
        out_shape=shape(groups * slab, LANES),
        in_specs=[VMEM] * (chord + 1) + [pl.BlockSpec(memory_space=pl.ANY)],
        out_specs=VMEM,
        compiler_params=params(),
        cost_estimate=pl.CostEstimate(flops=FIRST, bytes_accessed=1000000, transcendentals=0),
        name="keep",
    )(rel, messages[0], *wall_got, p1)

    own, *zs = pl.pallas_call(
        functools.partial(combine_kernel, slab),
        out_shape=(shape(slab, LANES),) + (shape(3 * slab, LANES),) * (groups - 1),
        in_specs=[VMEM] * 3,
        out_specs=(VMEM,) * groups,
        compiler_params=params(),
        name="combine",
    )(p1, p1_got, kept)
    z_got = [swap(zs[q - 1], "span", 2 * q) for q in range(1, groups)]

    flow1 = pl.pallas_call(
        functools.partial(stencil_kernel, span),
        out_shape=jax.ShapeDtypeStruct(flow_state.shape, F32),
        in_specs=[VMEM] * 6 + [pl.BlockSpec(memory_space=pl.ANY)],
        out_specs=VMEM,
        scratch_shapes=[
            pltpu.VMEM((4, nq, ccols, LANES), F32),
            pltpu.VMEM((2, nq, ccols, LANES), F32),
        ],
        compiler_params=params(),
        cost_estimate=pl.CostEstimate(
            flops=4 * 7 * nvar * nvar * srows * ccols * ncell,
            bytes_accessed=2 * jacobians.size + 8 * flow_state.size,
            transcendentals=0,
        ),
        name="stencil",
    )(flow_state, jacobians, near_got, far_got, lo, hi, own)

    flow_image, out = pl.pallas_call(
        functools.partial(couple_kernel, span),
        out_shape=(jax.ShapeDtypeStruct(flow_state.shape, F32), shape(ndof, nvec, sta_dev)),
        in_specs=[VMEM] * (8 + groups - 1),
        out_specs=(VMEM, VMEM),
        scratch_shapes=[
            pltpu.VMEM((span, rows, sta_dev), F32),
            pltpu.VMEM((rows, srows, ccols), F32),
        ],
        compiler_params=params(),
        cost_estimate=pl.CostEstimate(flops=20000000, bytes_accessed=6000000, transcendentals=0),
        name="couple",
    )(
        flow1, motion_map, maskf, rel, stiffness, p1, p1_got, own, *z_got
    )

    return flow_image, jnp.transpose(out, (1, 0, 2))


def solution(mesh):
    in_specs = (
        P(None, None, "span", "chord", None),
        P(None, None, None, "span", "chord", None),
        P(None, None, "span"),
        P(None, None, None, "span"),
        P(None, None, "span", "chord"),
        P(None, None, "span", "chord"),
        P("span", "chord"),
        P("span", "chord"),
    )
    out_specs = (P(None, None, "span", "chord", None), P(None, None, "span"))
    return jax.shard_map(
        on_device, mesh=mesh, in_specs=in_specs, out_specs=out_specs, check_vma=False
    )
```

```python
import functools

import jax
import jax.numpy as jnp
from jax import lax
from jax.experimental import pallas as pl
from jax.experimental.pallas import tpu as pltpu
from jax.sharding import PartitionSpec as P

F32 = jnp.float32
BF16 = jnp.bfloat16
LANES = 128
VMEM = pl.BlockSpec(memory_space=pltpu.VMEM)
LIMIT = 16 * 1024 * 1024
FIRST = 20000000000


def params():
    return pltpu.CompilerParams(vmem_limit_bytes=LIMIT)


def halves(x):
    hi = x.astype(BF16).astype(F32)
    return jnp.concatenate([hi, x - hi], axis=0).astype(BF16)


def lane_row(x, width):
    return jnp.concatenate([x[r : r + 1, :width] for r in range(x.shape[0])], axis=1)


def table(stations, count):
    rows = lax.broadcasted_iota(jnp.int32, (count, stations.shape[1]), 0)
    return (rows == (stations & (count - 1))).astype(F32).astype(BF16)


def in_group(stations, p, count):
    return ((stations >> (count.bit_length() - 1)) == p).astype(F32)


def put_slabs(ref, base, rows):
    n = rows.shape[0]
    for h in range(rows.shape[1] // LANES):
        ref[base + h * n : base + (h + 1) * n] = rows[:, h * LANES : (h + 1) * LANES]


def get_slabs(ref, base, n, k):
    return jnp.concatenate([ref[base + h * n : base + (h + 1) * n] for h in range(k)], axis=1)


def relative(sta, me, sta_dev, ccols):
    return lane_row(sta[...] ^ (me * sta_dev), ccols)


def face_kernel(flow, near, far, low, high, surf):
    nvec, nvar, srows, ccols, _ = flow.shape
    odd = lax.axis_index("span") % 2 == 1
    near_row = jnp.where(odd, 0, srows - 1)
    far_row = srows - 1 - near_row
    lane = lax.broadcasted_iota(jnp.int32, (ccols, LANES), 1)
    packed = jnp.zeros((ccols, LANES), F32)
    for v in range(nvec):
        for b in range(nvar):
            q = v * nvar + b
            near[q * ccols : (q + 1) * ccols] = flow[v, b, near_row]
            far[q * ccols : (q + 1) * ccols] = flow[v, b, far_row]
            low[q * srows : (q + 1) * srows] = flow[v, b, :, 0, :]
            high[q * srows : (q + 1) * srows] = flow[v, b, :, ccols - 1, :]
            for r in range(srows):
                at = q * 8 + r
                x = flow[v, b, r]
                if at:
                    x = pltpu.roll(x, at, 1)
                packed = jnp.where(lane == at, x, packed)
    surf[...] = packed.T


def neighbour_steps(chord):
    return [m for m in range(1, chord) if m & (m + 1) == 0]


def wall_kernel(chord, sta_dev, surf_in, lmap, mask, sta, low, high, *refs):
    messages, (rel, maskf_out, wall) = refs[: chord - 1], refs[chord - 1 :]
    rows = wall.shape[0]
    nvar = lmap.shape[1]
    ndof = lmap.shape[0]
    nvec = rows // ndof
    srows, ccols = mask.shape
    slab = rows * (srows * ccols // LANES)
    me = lax.axis_index("span")
    column = lax.axis_index("chord")
    surf = surf_in[...]
    maskf = mask[...].astype(F32)
    maskf_out[...] = maskf
    for v in range(nvec):
        near = [surf[(v * nvar + a) * 8 : (v * nvar + a) * 8 + srows] * maskf for a in range(nvar)]
        for j in range(ndof):
            total = lmap[j, 0] * near[0]
            for a in range(1, nvar):
                total = total + lmap[j, a] * near[a]
            wall[v * ndof + j] = total
    walls = jnp.concatenate([wall[:, r, :] for r in range(srows)], axis=1)
    stations = relative(sta, me, sta_dev, ccols)
    rel[...] = stations
    numbers = jnp.broadcast_to(stations.astype(F32), (8, stations.shape[1]))
    for m in range(1, chord):
        message = messages[m - 1]
        put_slabs(message, 0, walls)
        put_slabs(message, slab, numbers)
        if m in neighbour_steps(chord):
            base = slab + 8 * (walls.shape[1] // LANES)
            message[base:] = jnp.where((column ^ m) > column, high[...], low[...])


def dense_terms(span, first, rel, walls, rows, sta_dev, out):
    wide = rel.shape[1] // LANES
    k = sta_dev // LANES
    slab = rows * wide
    parts = [halves(get_slabs(x, 0, rows, wide)) for x in walls]
    stations = [rel[...]]
    for x in walls[1:]:
        stations.append(get_slabs(x, slab, 8, wide)[:1].astype(jnp.int32))
    groups = range(first, span, 2)
    both = 0.0
    for x, st in zip(parts, stations):
        spread = [x * in_group(st, p, sta_dev).astype(BF16) for p in groups]
        both = both + lax.dot_general(
            jnp.concatenate(spread, axis=0),
            table(st, sta_dev),
            (((1,), (1,)), ((), ())),
            preferred_element_type=F32,
        )
    for n in range(len(groups)):
        at = 2 * n * rows
        put_slabs(out, n * rows * k, both[at : at + rows] + both[at + rows : at + 2 * rows])


def send_kernel(span, chord, rel, beam, *refs):
    walls, (p1, lo, hi) = refs[:chord], refs[chord:]
    ndof, nvec, sta_dev = beam.shape
    k = sta_dev // LANES
    rows = nvec * ndof
    column = lax.axis_index("chord")
    dense_terms(span, 1, rel, walls, rows, sta_dev, p1)
    at0 = (span // 2) * rows * k
    for v in range(nvec):
        for j in range(ndof):
            for h in range(k):
                at = at0 + h * rows + v * ndof + j
                p1[at : at + 1] = beam[j, v : v + 1, h * LANES : (h + 1) * LANES]
    base = (rows + 8) * (rel.shape[1] // LANES)
    low, high = jnp.zeros(lo.shape, F32), jnp.zeros(hi.shape, F32)
    for m in neighbour_steps(chord):
        x = walls[m][base:]
        low = jnp.where((column > 0) & ((column ^ (column - 1)) == m), x, low)
        high = jnp.where((column < chord - 1) & ((column ^ (column + 1)) == m), x, high)
    lo[...] = low
    hi[...] = high


def keep_kernel(span, chord, rows, sta_dev, rel, *refs):
    walls, kept = refs[:chord], refs[-1]
    dense_terms(span, 0, rel, walls, rows, sta_dev, kept)


def combine_kernel(slab, sent, got, kept, own, *out):
    groups = len(out) + 1
    base = groups * slab
    own[...] = kept[:slab] + got[:slab]
    for q in range(1, groups):
        o = out[q - 1]
        o[:slab] = kept[q * slab : (q + 1) * slab] + got[q * slab : (q + 1) * slab]
        o[slab : 2 * slab] = sent[base : base + slab]
        o[2 * slab :] = got[base : base + slab]


def stencil_kernel(span, flow, jac, got, far, lo, hi, _, out, padded, faces):
    nvec, nvar, srows, ccols, _ = flow.shape
    me = lax.axis_index("span")
    odd = me % 2
    inner = jnp.where((me > 0) & (me < span - 1), 1.0, 0.0).astype(F32)
    tile = 16
    lane = lax.broadcasted_iota(jnp.int32, (tile, LANES), 1)
    for q in range(nvec * nvar):
        one, two = got[q * ccols : (q + 1) * ccols], far[q * ccols : (q + 1) * ccols] * inner
        faces[0, q] = jnp.where(odd == 1, one, two)
        faces[1, q] = jnp.where(odd == 1, two, one)

    def one_row(r, carry):
        for v in range(nvec):
            for b in range(nvar):
                q = v * nvar + b
                padded[q, 8 : 8 + ccols] = flow[v, b, r]
                padded[q, 7:8] = lo[pl.ds(q * srows + r, 1)]
                padded[q, 8 + ccols : 9 + ccols] = hi[pl.ds(q * srows + r, 1)]
        first, last = r == 0, r == srows - 1
        below = jnp.where(first, 0, r - 1)
        above = jnp.where(last, srows - 1, r + 1)
        for c in range(0, ccols, tile):
            here = slice(c, c + tile)

            def value(e, v, b):
                q = v * nvar + b
                if e == 1:
                    return jnp.where(first, faces[0, q, here], flow[v, b, below, here])
                if e == 2:
                    return jnp.where(last, faces[1, q, here], flow[v, b, above, here])
                if e == 3:
                    return padded[q, c + 7 : c + 7 + tile]
                if e == 4:
                    return padded[q, c + 9 : c + 9 + tile]
                x = flow[v, b, r, here]
                if e == 5:
                    return jnp.where(lane == 0, 0.0, pltpu.roll(x, 1, 1))
                if e == 6:
                    return jnp.where(lane == LANES - 1, 0.0, pltpu.roll(x, LANES - 1, 1))
                return x

            acc = [[jnp.zeros((tile, LANES), F32) for _ in range(nvar)] for _ in range(nvec)]
            for b in range(nvar):
                for e in (0, 5, 6, 1, 2, 3, 4):
                    xs = [value(e, v, b) for v in range(nvec)]
                    for a in range(nvar):
                        m = jac[e, a, b, r, here].astype(F32)
                        for v in range(nvec):
                            acc[v][a] = acc[v][a] + m * xs[v]
            for v in range(nvec):
                for a in range(nvar):
                    out[v, a, r, here] = acc[v][a]
        return carry

    lax.fori_loop(0, srows, one_row, 0)


def couple_kernel(
    span, flow_in, motion, mask, rel, stiff, sent, got, own_loads, *rest
):
    groups = span // 2
    zs = rest[: groups - 1][::-1]
    flow, beam_out, gath, lk = rest[groups - 1 :]
    nvec, nvar, srows, ccols, _ = flow_in.shape
    _, ndof, _, sta_dev = stiff.shape
    k = sta_dev // LANES
    rows = nvec * ndof
    slab = rows * k
    me = lax.axis_index("span")
    base = groups * slab
    gath[0] = get_slabs(sent, base, rows, k)
    gath[1] = get_slabs(got, base, rows, k)
    for q in range(1, groups):
        gath[2 * q] = get_slabs(zs[q - 1], slab, rows, k)
        gath[2 * q + 1] = get_slabs(zs[q - 1], 2 * slab, rows, k)
    stations = rel[...]
    beams = jnp.concatenate([halves(gath[p]) for p in range(span)], axis=0)
    each = jnp.dot(beams, table(stations, sta_dev), preferred_element_type=F32)
    looked = jnp.zeros((rows, srows * ccols), F32)
    for p in range(span):
        at = 2 * p * rows
        both = each[at : at + rows] + each[at + rows : at + 2 * rows]
        looked = looked + both * in_group(stations, p, sta_dev)
    for r in range(srows):
        lk[:, r, :] = looked[:, r * ccols : (r + 1) * ccols]
    maskf = mask[...]
    tiles = []
    for v in range(nvec):
        for a in range(nvar):
            total = motion[a, 0] * lk[v * ndof]
            for j in range(1, ndof):
                total = total + motion[a, j] * lk[v * ndof + j]
            total = total * maskf
            tiles.append(jnp.concatenate([total, jnp.zeros((8 - srows, ccols), F32)], axis=0))
    tiles.append(jnp.zeros((LANES - 8 * len(tiles), ccols), F32))
    packed = jnp.concatenate(tiles, axis=0).T
    lane = lax.broadcasted_iota(jnp.int32, (ccols, LANES), 1)
    for v in range(nvec):
        for a in range(nvar):
            for r in range(srows):
                at = (v * nvar + a) * 8 + r
                x = packed if at == 0 else pltpu.roll(packed, LANES - at, 1)
                flow[v, a, r] = flow_in[v, a, r] + jnp.where(lane == 0, x, 0.0)
    own = gath[0]
    before = gath[jnp.where(me > 0, me ^ (me - 1), 0)]
    after = gath[jnp.where(me < span - 1, me ^ (me + 1), 0)]
    pos = lax.broadcasted_iota(jnp.int32, (rows, sta_dev), 1)
    place = pos + me * sta_dev
    stations_all = span * sta_dev
    blade_len = stations_all // 4

    def blade(t):
        n = jnp.zeros(t.shape, jnp.int32)
        for m in range(1, 5):
            n = n + (t + sta_dev // 2 >= m * blade_len).astype(jnp.int32)
        return n

    home = blade(place)
    shifted = []
    for d in range(5):
        s = d - 2
        other = place + s
        x = own if s == 0 else pltpu.roll(own, (-s) % sta_dev, 1)
        if s < 0:
            x = jnp.where(pos < -s, pltpu.roll(before, -s, 1), x)
        if s > 0:
            x = jnp.where(pos >= sta_dev - s, pltpu.roll(after, sta_dev - s, 1), x)
        good = (blade(other) == home) & (other >= 0) & (other < stations_all)
        x = jnp.where(good, x, 0.0)
        shifted.append([x[v * ndof : (v + 1) * ndof] for v in range(nvec)])
    loads = own_loads[...]
    for z in zs:
        loads = loads + z[:slab]
    loads = jnp.concatenate([loads[h * rows : (h + 1) * rows] for h in range(k)], axis=1)
    for i in range(ndof):
        for v in range(nvec):
            total = stiff[0, i] * shifted[0][v]
            for d in range(1, 5):
                total = total + stiff[d, i] * shifted[d][v]
            at = v * ndof + i
            beam_out[i, v : v + 1, :] = jnp.sum(total, axis=0, keepdims=True) - loads[at : at + 1]


def swap(x, axis, m):
    return lax.ppermute(x, axis, [(i, i ^ m) for i in range(lax.axis_size(axis))])


def far_pairs(span, chord):
    pairs = []
    for i in range(span):
        for c in range(chord):
            if 0 < i < span - 1:
                to = (i + 1 if i % 2 else i - 1, c)
            else:
                to = (i, c ^ 1)
            pairs.append((i * chord + c, to[0] * chord + to[1]))
    return pairs


def on_device(
    flow_state, jacobians, beam_state, stiffness, motion_map, load_map, surface_mask, station_of
):
    nvec, nvar, srows, ccols, ncell = flow_state.shape
    ndof, sta_dev = beam_state.shape[1:]
    span, chord = lax.axis_size("span"), lax.axis_size("chord")
    groups = span // 2
    k = sta_dev // LANES
    rows = nvec * ndof
    slab = rows * k
    halo = nvec * nvar * ccols
    nq = nvec * nvar
    beam = jnp.transpose(beam_state, (1, 0, 2))

    def shape(*s):
        return jax.ShapeDtypeStruct(s, F32)

    near, far, low, high, surf = pl.pallas_call(
        face_kernel,
        out_shape=(
            shape(halo, LANES),
            shape(halo, LANES),
            shape(nq * srows, LANES),
            shape(nq * srows, LANES),
            shape(LANES, ccols),
        ),
        in_specs=[VMEM],
        out_specs=(VMEM,) * 5,
        compiler_params=params(),
        cost_estimate=pl.CostEstimate(flops=FIRST, bytes_accessed=2000000, transcendentals=0),
        name="faces",
    )(flow_state)
    near_got = swap(near, "span", 1)
    far_got = lax.ppermute(far, ("span", "chord"), far_pairs(span, chord))

    wide = srows * ccols // LANES
    wall_rows = (rows + 8) * wide
    message_rows = [
        wall_rows + (nq * srows if m in neighbour_steps(chord) else 0) for m in range(1, chord)
    ]
    *messages, rel, maskf = pl.pallas_call(
        functools.partial(wall_kernel, chord, sta_dev),
        out_shape=tuple(shape(n, LANES) for n in message_rows)
        + (jax.ShapeDtypeStruct((1, srows * ccols), jnp.int32), shape(srows, ccols)),
        in_specs=[VMEM] * 6,
        out_specs=(VMEM,) * (chord + 1),
        scratch_shapes=[pltpu.VMEM((rows, srows, ccols), F32)],
        compiler_params=params(),
        cost_estimate=pl.CostEstimate(flops=FIRST, bytes_accessed=1000000, transcendentals=0),
        name="wall",
    )(surf, load_map, surface_mask, station_of, low, high)
    wall_got = [swap(messages[m - 1], "chord", m) for m in range(1, chord)]

    p1, lo, hi = pl.pallas_call(
        functools.partial(send_kernel, span, chord),
        out_shape=(
            shape((groups + 1) * slab, LANES),
            shape(nq * srows, LANES),
            shape(nq * srows, LANES),
        ),
        in_specs=[VMEM] * (chord + 2),
        out_specs=(VMEM,) * 3,
        compiler_params=params(),
        cost_estimate=pl.CostEstimate(flops=FIRST, bytes_accessed=1000000, transcendentals=0),
        name="send",
    )(rel, beam, messages[0], *wall_got)
    p1_got = swap(p1, "span", 1)
    kept = pl.pallas_call(
        functools.partial(keep_kernel, span, chord, rows, sta_dev),
        out_shape=shape(groups * slab, LANES),
        in_specs=[VMEM] * (chord + 1) + [pl.BlockSpec(memory_space=pl.ANY)],
        out_specs=VMEM,
        compiler_params=params(),
        cost_estimate=pl.CostEstimate(flops=FIRST, bytes_accessed=1000000, transcendentals=0),
        name="keep",
    )(rel, messages[0], *wall_got, p1)

    own, *zs = pl.pallas_call(
        functools.partial(combine_kernel, slab),
        out_shape=(shape(slab, LANES),) + (shape(3 * slab, LANES),) * (groups - 1),
        in_specs=[VMEM] * 3,
        out_specs=(VMEM,) * groups,
        compiler_params=params(),
        name="combine",
    )(p1, p1_got, kept)
    z_got = [swap(zs[q - 1], "span", 2 * q) for q in range(1, groups)]

    flow1 = pl.pallas_call(
        functools.partial(stencil_kernel, span),
        out_shape=jax.ShapeDtypeStruct(flow_state.shape, F32),
        in_specs=[VMEM] * 6 + [pl.BlockSpec(memory_space=pl.ANY)],
        out_specs=VMEM,
        scratch_shapes=[
            pltpu.VMEM((nq, ccols + 16, LANES), F32),
            pltpu.VMEM((2, nq, ccols, LANES), F32),
        ],
        compiler_params=params(),
        cost_estimate=pl.CostEstimate(
            flops=4 * 7 * nvar * nvar * srows * ccols * ncell,
            bytes_accessed=2 * jacobians.size + 8 * flow_state.size,
            transcendentals=0,
        ),
        name="stencil",
    )(flow_state, jacobians, near_got, far_got, lo, hi, own)

    flow_image, out = pl.pallas_call(
        functools.partial(couple_kernel, span),
        out_shape=(jax.ShapeDtypeStruct(flow_state.shape, F32), shape(ndof, nvec, sta_dev)),
        in_specs=[VMEM] * (8 + groups - 1),
        out_specs=(VMEM, VMEM),
        scratch_shapes=[
            pltpu.VMEM((span, rows, sta_dev), F32),
            pltpu.VMEM((rows, srows, ccols), F32),
        ],
        compiler_params=params(),
        cost_estimate=pl.CostEstimate(flops=20000000, bytes_accessed=6000000, transcendentals=0),
        name="couple",
    )(
        flow1, motion_map, maskf, rel, stiffness, p1, p1_got, own, *z_got[::-1]
    )

    return flow_image, jnp.transpose(out, (1, 0, 2))


def solution(mesh):
    in_specs = (
        P(None, None, "span", "chord", None),
        P(None, None, None, "span", "chord", None),
        P(None, None, "span"),
        P(None, None, None, "span"),
        P(None, None, "span", "chord"),
        P(None, None, "span", "chord"),
        P("span", "chord"),
        P("span", "chord"),
    )
    out_specs = (P(None, None, "span", "chord", None), P(None, None, "span"))
    return jax.shard_map(
        on_device, mesh=mesh, in_specs=in_specs, out_specs=out_specs, check_vma=False
    )
```

```python
import functools

import jax
import jax.numpy as jnp
from jax import lax
from jax.experimental import pallas as pl
from jax.experimental.pallas import tpu as pltpu
from jax.sharding import PartitionSpec as P

F32 = jnp.float32
BF16 = jnp.bfloat16
LANES = 128
VMEM = pl.BlockSpec(memory_space=pltpu.VMEM)
LIMIT = 16 * 1024 * 1024
FIRST = 20000000000


def params():
    return pltpu.CompilerParams(vmem_limit_bytes=LIMIT)


def halves(x):
    hi = x.astype(BF16).astype(F32)
    return jnp.concatenate([hi, x - hi], axis=0).astype(BF16)


def lane_row(x, width):
    return jnp.concatenate([x[r : r + 1, :width] for r in range(x.shape[0])], axis=1)


def table(stations, count):
    rows = lax.broadcasted_iota(jnp.int32, (count, stations.shape[1]), 0)
    return (rows == (stations & (count - 1))).astype(F32).astype(BF16)


def in_group(stations, p, count):
    return ((stations >> (count.bit_length() - 1)) == p).astype(F32)


def put_slabs(ref, base, rows):
    n = rows.shape[0]
    for h in range(rows.shape[1] // LANES):
        ref[base + h * n : base + (h + 1) * n] = rows[:, h * LANES : (h + 1) * LANES]


def get_slabs(ref, base, n, k):
    return jnp.concatenate([ref[base + h * n : base + (h + 1) * n] for h in range(k)], axis=1)


def relative(sta, me, sta_dev, ccols):
    return lane_row(sta[...] ^ (me * sta_dev), ccols)


def face_kernel(flow, near, far, low, high, surf):
    nvec, nvar, srows, ccols, _ = flow.shape
    odd = lax.axis_index("span") % 2 == 1
    near_row = jnp.where(odd, 0, srows - 1)
    far_row = srows - 1 - near_row
    lane = lax.broadcasted_iota(jnp.int32, (ccols, LANES), 1)
    packed = jnp.zeros((ccols, LANES), F32)
    for v in range(nvec):
        for b in range(nvar):
            q = v * nvar + b
            near[q * ccols : (q + 1) * ccols] = flow[v, b, near_row]
            far[q * ccols : (q + 1) * ccols] = flow[v, b, far_row]
            low[q * srows : (q + 1) * srows] = flow[v, b, :, 0, :]
            high[q * srows : (q + 1) * srows] = flow[v, b, :, ccols - 1, :]
            for r in range(srows):
                at = q * 8 + r
                x = flow[v, b, r]
                if at:
                    x = pltpu.roll(x, at, 1)
                packed = jnp.where(lane == at, x, packed)
    surf[...] = packed.T


def neighbour_steps(chord):
    return [m for m in range(1, chord) if m & (m + 1) == 0]


def wall_kernel(chord, sta_dev, surf_in, lmap, mask, sta, low, high, *refs):
    messages, (rel, maskf_out, wall) = refs[: chord - 1], refs[chord - 1 :]
    rows = wall.shape[0]
    nvar = lmap.shape[1]
    ndof = lmap.shape[0]
    nvec = rows // ndof
    srows, ccols = mask.shape
    slab = rows * (srows * ccols // LANES)
    me = lax.axis_index("span")
    column = lax.axis_index("chord")
    surf = surf_in[...]
    maskf = mask[...].astype(F32)
    maskf_out[...] = maskf
    for v in range(nvec):
        near = [surf[(v * nvar + a) * 8 : (v * nvar + a) * 8 + srows] * maskf for a in range(nvar)]
        for j in range(ndof):
            total = lmap[j, 0] * near[0]
            for a in range(1, nvar):
                total = total + lmap[j, a] * near[a]
            wall[v * ndof + j] = total
    walls = jnp.concatenate([wall[:, r, :] for r in range(srows)], axis=1)
    stations = relative(sta, me, sta_dev, ccols)
    rel[...] = stations
    wide = stations.shape[1] // LANES
    for m in range(1, chord):
        message = messages[m - 1]
        put_slabs(message, 0, walls)
        put_slabs(message, slab, stations.astype(F32))
        message[slab + wide : slab + 8] = jnp.zeros((8 - wide, LANES), F32)
        if m in neighbour_steps(chord):
            message[slab + 8 :] = jnp.where((column ^ m) > column, high[...], low[...])


def dense_terms(span, first, rel, walls, rows, sta_dev, out):
    wide = rel.shape[1] // LANES
    k = sta_dev // LANES
    slab = rows * wide
    parts = [halves(get_slabs(x, 0, rows, wide)) for x in walls]
    stations = [rel[...]]
    for x in walls[1:]:
        stations.append(get_slabs(x, slab, 1, wide).astype(jnp.int32))
    groups = range(first, span, 2)
    both = 0.0
    for x, st in zip(parts, stations):
        spread = [x * in_group(st, p, sta_dev).astype(BF16) for p in groups]
        both = both + lax.dot_general(
            jnp.concatenate(spread, axis=0),
            table(st, sta_dev),
            (((1,), (1,)), ((), ())),
            preferred_element_type=F32,
        )
    for n in range(len(groups)):
        at = 2 * n * rows
        put_slabs(out, n * rows * k, both[at : at + rows] + both[at + rows : at + 2 * rows])


def send_kernel(span, chord, rel, beam, *refs):
    walls, (p1, lo, hi) = refs[:chord], refs[chord:]
    ndof, nvec, sta_dev = beam.shape
    k = sta_dev // LANES
    rows = nvec * ndof
    column = lax.axis_index("chord")
    dense_terms(span, 1, rel, walls, rows, sta_dev, p1)
    at0 = (span // 2) * rows * k
    for v in range(nvec):
        for j in range(ndof):
            for h in range(k):
                at = at0 + h * rows + v * ndof + j
                p1[at : at + 1] = beam[j, v : v + 1, h * LANES : (h + 1) * LANES]
    base = rows * (rel.shape[1] // LANES) + 8
    low, high = jnp.zeros(lo.shape, F32), jnp.zeros(hi.shape, F32)
    for m in neighbour_steps(chord):
        x = walls[m][base:]
        low = jnp.where((column > 0) & ((column ^ (column - 1)) == m), x, low)
        high = jnp.where((column < chord - 1) & ((column ^ (column + 1)) == m), x, high)
    lo[...] = low
    hi[...] = high


def keep_kernel(span, chord, rows, sta_dev, rel, *refs):
    walls, kept = refs[:chord], refs[-1]
    dense_terms(span, 0, rel, walls, rows, sta_dev, kept)


def combine_kernel(slab, sent, got, kept, own, *out):
    groups = len(out) + 1
    base = groups * slab
    own[...] = kept[:slab] + got[:slab]
    for q in range(1, groups):
        o = out[q - 1]
        o[:slab] = kept[q * slab : (q + 1) * slab] + got[q * slab : (q + 1) * slab]
        o[slab : 2 * slab] = sent[base : base + slab]
        o[2 * slab :] = got[base : base + slab]


def stencil_kernel(span, flow, jac, got, far, lo, hi, _, out, padded, faces):
    nvec, nvar, srows, ccols, _ = flow.shape
    me = lax.axis_index("span")
    odd = me % 2
    inner = jnp.where((me > 0) & (me < span - 1), 1.0, 0.0).astype(F32)
    tile = 16
    lane = lax.broadcasted_iota(jnp.int32, (tile, LANES), 1)
    for q in range(nvec * nvar):
        one, two = got[q * ccols : (q + 1) * ccols], far[q * ccols : (q + 1) * ccols] * inner
        faces[0, q] = jnp.where(odd == 1, one, two)
        faces[1, q] = jnp.where(odd == 1, two, one)

    def one_row(r, carry):
        for v in range(nvec):
            for b in range(nvar):
                q = v * nvar + b
                padded[q, 8 : 8 + ccols] = flow[v, b, r]
                padded[q, 7:8] = lo[pl.ds(q * srows + r, 1)]
                padded[q, 8 + ccols : 9 + ccols] = hi[pl.ds(q * srows + r, 1)]
        first, last = r == 0, r == srows - 1
        below = jnp.where(first, 0, r - 1)
        above = jnp.where(last, srows - 1, r + 1)
        for c in range(0, ccols, tile):
            here = slice(c, c + tile)

            def value(e, v, b):
                q = v * nvar + b
                if e == 1:
                    return jnp.where(first, faces[0, q, here], flow[v, b, below, here])
                if e == 2:
                    return jnp.where(last, faces[1, q, here], flow[v, b, above, here])
                if e == 3:
                    return padded[q, c + 7 : c + 7 + tile]
                if e == 4:
                    return padded[q, c + 9 : c + 9 + tile]
                x = flow[v, b, r, here]
                if e == 5:
                    return jnp.where(lane == 0, 0.0, pltpu.roll(x, 1, 1))
                if e == 6:
                    return jnp.where(lane == LANES - 1, 0.0, pltpu.roll(x, LANES - 1, 1))
                return x

            acc = [[jnp.zeros((tile, LANES), F32) for _ in range(nvar)] for _ in range(nvec)]
            for b in range(nvar):
                for e in (0, 5, 6, 1, 2, 3, 4):
                    xs = [value(e, v, b) for v in range(nvec)]
                    for a in range(nvar):
                        m = jac[e, a, b, r, here].astype(F32)
                        for v in range(nvec):
                            acc[v][a] = acc[v][a] + m * xs[v]
            for v in range(nvec):
                for a in range(nvar):
                    out[v, a, r, here] = acc[v][a]
        return carry

    lax.fori_loop(0, srows, one_row, 0)


def couple_kernel(
    span, flow_in, motion, mask, rel, stiff, sent, got, own_loads, *rest
):
    groups = span // 2
    order = z_order(groups)
    zs = [rest[order.index(q)] for q in range(1, groups)]
    flow, beam_out, gath, lk = rest[groups - 1 :]
    nvec, nvar, srows, ccols, _ = flow_in.shape
    _, ndof, _, sta_dev = stiff.shape
    k = sta_dev // LANES
    rows = nvec * ndof
    slab = rows * k
    me = lax.axis_index("span")
    base = groups * slab
    gath[0] = get_slabs(sent, base, rows, k)
    gath[1] = get_slabs(got, base, rows, k)
    for q in range(1, groups):
        gath[2 * q] = get_slabs(zs[q - 1], slab, rows, k)
        gath[2 * q + 1] = get_slabs(zs[q - 1], 2 * slab, rows, k)
    stations = rel[...]
    beams = jnp.concatenate([halves(gath[p]) for p in range(span)], axis=0)
    each = jnp.dot(beams, table(stations, sta_dev), preferred_element_type=F32)
    looked = jnp.zeros((rows, srows * ccols), F32)
    for p in range(span):
        at = 2 * p * rows
        both = each[at : at + rows] + each[at + rows : at + 2 * rows]
        looked = looked + both * in_group(stations, p, sta_dev)
    for r in range(srows):
        lk[:, r, :] = looked[:, r * ccols : (r + 1) * ccols]
    maskf = mask[...]
    tiles = []
    for v in range(nvec):
        for a in range(nvar):
            total = motion[a, 0] * lk[v * ndof]
            for j in range(1, ndof):
                total = total + motion[a, j] * lk[v * ndof + j]
            total = total * maskf
            tiles.append(jnp.concatenate([total, jnp.zeros((8 - srows, ccols), F32)], axis=0))
    tiles.append(jnp.zeros((LANES - 8 * len(tiles), ccols), F32))
    packed = jnp.concatenate(tiles, axis=0).T
    lane = lax.broadcasted_iota(jnp.int32, (ccols, LANES), 1)
    for v in range(nvec):
        for a in range(nvar):
            for r in range(srows):
                at = (v * nvar + a) * 8 + r
                x = packed if at == 0 else pltpu.roll(packed, LANES - at, 1)
                flow[v, a, r] = flow_in[v, a, r] + jnp.where(lane == 0, x, 0.0)
    own = gath[0]
    before = gath[jnp.where(me > 0, me ^ (me - 1), 0)]
    after = gath[jnp.where(me < span - 1, me ^ (me + 1), 0)]
    pos = lax.broadcasted_iota(jnp.int32, (rows, sta_dev), 1)
    place = pos + me * sta_dev
    stations_all = span * sta_dev
    blade_len = stations_all // 4

    def blade(t):
        n = jnp.zeros(t.shape, jnp.int32)
        for m in range(1, 5):
            n = n + (t + sta_dev // 2 >= m * blade_len).astype(jnp.int32)
        return n

    home = blade(place)
    shifted = []
    for d in range(5):
        s = d - 2
        other = place + s
        x = own if s == 0 else pltpu.roll(own, (-s) % sta_dev, 1)
        if s < 0:
            x = jnp.where(pos < -s, pltpu.roll(before, -s, 1), x)
        if s > 0:
            x = jnp.where(pos >= sta_dev - s, pltpu.roll(after, sta_dev - s, 1), x)
        good = (blade(other) == home) & (other >= 0) & (other < stations_all)
        x = jnp.where(good, x, 0.0)
        shifted.append([x[v * ndof : (v + 1) * ndof] for v in range(nvec)])
    loads = own_loads[...]
    for z in zs:
        loads = loads + z[:slab]
    loads = jnp.concatenate([loads[h * rows : (h + 1) * rows] for h in range(k)], axis=1)
    for i in range(ndof):
        for v in range(nvec):
            total = stiff[0, i] * shifted[0][v]
            for d in range(1, 5):
                total = total + stiff[d, i] * shifted[d][v]
            at = v * ndof + i
            beam_out[i, v : v + 1, :] = jnp.sum(total, axis=0, keepdims=True) - loads[at : at + 1]


def z_order(groups):
    half = groups // 2
    return [q for q in range(1, groups) if q >= half] + [q for q in range(1, groups) if q < half]


def swap(x, axis, m):
    return lax.ppermute(x, axis, [(i, i ^ m) for i in range(lax.axis_size(axis))])


def far_pairs(span, chord):
    pairs = []
    for i in range(span):
        for c in range(chord):
            if 0 < i < span - 1:
                to = (i + 1 if i % 2 else i - 1, c)
            else:
                to = (i, c ^ 1)
            pairs.append((i * chord + c, to[0] * chord + to[1]))
    return pairs


def on_device(
    flow_state, jacobians, beam_state, stiffness, motion_map, load_map, surface_mask, station_of
):
    nvec, nvar, srows, ccols, ncell = flow_state.shape
    ndof, sta_dev = beam_state.shape[1:]
    span, chord = lax.axis_size("span"), lax.axis_size("chord")
    groups = span // 2
    k = sta_dev // LANES
    rows = nvec * ndof
    slab = rows * k
    halo = nvec * nvar * ccols
    nq = nvec * nvar
    beam = jnp.transpose(beam_state, (1, 0, 2))

    def shape(*s):
        return jax.ShapeDtypeStruct(s, F32)

    near, far, low, high, surf = pl.pallas_call(
        face_kernel,
        out_shape=(
            shape(halo, LANES),
            shape(halo, LANES),
            shape(nq * srows, LANES),
            shape(nq * srows, LANES),
            shape(LANES, ccols),
        ),
        in_specs=[VMEM],
        out_specs=(VMEM,) * 5,
        compiler_params=params(),
        cost_estimate=pl.CostEstimate(flops=FIRST, bytes_accessed=2000000, transcendentals=0),
        name="faces",
    )(flow_state)
    near_got = swap(near, "span", 1)
    far_got = lax.ppermute(far, ("span", "chord"), far_pairs(span, chord))

    wide = srows * ccols // LANES
    wall_rows = rows * wide + 8
    message_rows = [
        wall_rows + (nq * srows if m in neighbour_steps(chord) else 0) for m in range(1, chord)
    ]
    *messages, rel, maskf = pl.pallas_call(
        functools.partial(wall_kernel, chord, sta_dev),
        out_shape=tuple(shape(n, LANES) for n in message_rows)
        + (jax.ShapeDtypeStruct((1, srows * ccols), jnp.int32), shape(srows, ccols)),
        in_specs=[VMEM] * 6,
        out_specs=(VMEM,) * (chord + 1),
        scratch_shapes=[pltpu.VMEM((rows, srows, ccols), F32)],
        compiler_params=params(),
        cost_estimate=pl.CostEstimate(flops=FIRST, bytes_accessed=1000000, transcendentals=0),
        name="wall",
    )(surf, load_map, surface_mask, station_of, low, high)
    wall_got = [swap(messages[m - 1], "chord", m) for m in range(1, chord)]

    p1, lo, hi = pl.pallas_call(
        functools.partial(send_kernel, span, chord),
        out_shape=(
            shape((groups + 1) * slab, LANES),
            shape(nq * srows, LANES),
            shape(nq * srows, LANES),
        ),
        in_specs=[VMEM] * (chord + 2),
        out_specs=(VMEM,) * 3,
        compiler_params=params(),
        cost_estimate=pl.CostEstimate(flops=FIRST, bytes_accessed=1000000, transcendentals=0),
        name="send",
    )(rel, beam, messages[0], *wall_got)
    p1_got = swap(p1, "span", 1)
    kept = pl.pallas_call(
        functools.partial(keep_kernel, span, chord, rows, sta_dev),
        out_shape=shape(groups * slab, LANES),
        in_specs=[VMEM] * (chord + 1) + [pl.BlockSpec(memory_space=pl.ANY)],
        out_specs=VMEM,
        compiler_params=params(),
        cost_estimate=pl.CostEstimate(flops=FIRST, bytes_accessed=1000000, transcendentals=0),
        name="keep",
    )(rel, messages[0], *wall_got, p1)

    own, *zs = pl.pallas_call(
        functools.partial(combine_kernel, slab),
        out_shape=(shape(slab, LANES),) + (shape(3 * slab, LANES),) * (groups - 1),
        in_specs=[VMEM] * 3,
        out_specs=(VMEM,) * groups,
        compiler_params=params(),
        name="combine",
    )(p1, p1_got, kept)
    z_got = [swap(zs[q - 1], "span", 2 * q) for q in range(1, groups)]

    flow1 = pl.pallas_call(
        functools.partial(stencil_kernel, span),
        out_shape=jax.ShapeDtypeStruct(flow_state.shape, F32),
        in_specs=[VMEM] * 6 + [pl.BlockSpec(memory_space=pl.ANY)],
        out_specs=VMEM,
        scratch_shapes=[
            pltpu.VMEM((nq, ccols + 16, LANES), F32),
            pltpu.VMEM((2, nq, ccols, LANES), F32),
        ],
        compiler_params=params(),
        cost_estimate=pl.CostEstimate(
            flops=4 * 7 * nvar * nvar * srows * ccols * ncell,
            bytes_accessed=2 * jacobians.size + 8 * flow_state.size,
            transcendentals=0,
        ),
        name="stencil",
    )(flow_state, jacobians, near_got, far_got, lo, hi, own)

    flow_image, out = pl.pallas_call(
        functools.partial(couple_kernel, span),
        out_shape=(jax.ShapeDtypeStruct(flow_state.shape, F32), shape(ndof, nvec, sta_dev)),
        in_specs=[VMEM] * (8 + groups - 1),
        out_specs=(VMEM, VMEM),
        scratch_shapes=[
            pltpu.VMEM((span, rows, sta_dev), F32),
            pltpu.VMEM((rows, srows, ccols), F32),
        ],
        compiler_params=params(),
        cost_estimate=pl.CostEstimate(flops=20000000, bytes_accessed=6000000, transcendentals=0),
        name="couple",
    )(
        flow1, motion_map, maskf, rel, stiffness, p1, p1_got, own, *[z_got[q - 1] for q in z_order(groups)]
    )

    return flow_image, jnp.transpose(out, (1, 0, 2))


def solution(mesh):
    in_specs = (
        P(None, None, "span", "chord", None),
        P(None, None, None, "span", "chord", None),
        P(None, None, "span"),
        P(None, None, None, "span"),
        P(None, None, "span", "chord"),
        P(None, None, "span", "chord"),
        P("span", "chord"),
        P("span", "chord"),
    )
    out_specs = (P(None, None, "span", "chord", None), P(None, None, "span"))
    return jax.shard_map(
        on_device, mesh=mesh, in_specs=in_specs, out_specs=out_specs, check_vma=False
    )
```
